256 devices in a mesh: feat: 16 (over y, x_hi, core), tok: 16 (over x_lo, z).
Axes of the slice: x: 4 (x_hi: 2, x_lo: 2; x = x_hi * 2 + x_lo), y: 4, z: 8, core: 2. Of those that a mesh axis runs over, the one named last changes fastest.
Arguments:
- key_rows: bfloat16 [2, 2048, 2048], P(None, 'tok'), may hold values from -6 to 6
- value_rows: bfloat16 [2, 2048, 2048], P(None, 'tok', 'feat'), may hold values from -6 to 6
- queries: bfloat16 [2, 2048, 2048], P(None, 'tok'), may hold values from -6 to 6
- output_cot: bfloat16 [2, 2048, 2048], P(None, 'tok'), may hold values from -3 to 3
- token_rates: float32 [2, 2048], P(None, 'tok'), may hold values from 0.002 to 0.02
- w_first: bfloat16 [2, 2048, 8192], P(None, None, 'feat'), may hold values from -0.125 to 0.125
- w_second: bfloat16 [2, 2048, 8192], P(None, None, 'feat'), may hold values from -0.0625 to 0.0625
- final_first: bfloat16 [2048, 8192], P('tok', 'feat'), may hold values from -24 to 24
- final_second: bfloat16 [2048, 8192], P('tok', 'feat'), may hold values from -24 to 24
Outputs:
- grad_keys: bfloat16 [2, 2048, 2048], P(None, 'tok', 'feat')
- grad_values: bfloat16 [2, 2048, 2048], P(None, 'tok', 'feat')
- grad_queries: bfloat16 [2, 2048, 2048], P(None, 'tok', 'feat')
- grad_first: float32 [2048, 8192], P('tok', 'feat')
- grad_second: float32 [2048, 8192], P('tok', 'feat')
The draws below stay inside these ranges and needn't reach their ends.
All inputs are finite; a program needn't handle non-finite values.
Results may differ from the reference program's by a relative error of at most 0.0095.
Values may be sent and summed in bfloat16 or wider, within the bound.
No kernel may reach another device: no remote copies, remote signals or barrier semaphores. Data moves between devices by JAX's collectives and lax.ppermute only.
A program may use at most 128 MiB of HBM per device.

```python
import math
import jax
import jax.numpy as jnp
from jax import lax

D = 2048
H = 8192
ROWS = 128
UPDATES = 2
BLOCK_LEN = 2048
N_TOK = 16


def level_of(rng, shape, shards, least, top_value):
    def one(position, shards_of):
        steps = jax.random.uniform(jax.random.fold_in(jax.random.fold_in(rng, 6), position), (shards_of,), jnp.float32, least / len(shards), top_value / len(shards))
        return jnp.repeat(jnp.exp(steps), shape[position] // shards_of).reshape((-1,) + (1,) * (len(shape) - position - 1))

    factor_of = one(*shards[0])
    for cut in shards[1:]:
        factor_of = factor_of * one(*cut)
    return factor_of


def noise(own_key, shape, scale, reach, shards=(), held_as=jnp.bfloat16):
    array = jax.random.normal(own_key, shape, jnp.float32) * scale
    if len(shards) > 0:
        array = level_of(own_key, shape, shards, -0.22, 0.18) * array
    return jnp.clip(array, min=-reach, max=reach).astype(held_as)


def setup_inputs(seed: int = 0) -> dict:
    streams_of = jax.random.split(jax.random.key(seed), 10)
    key_rows = noise(streams_of[0], (UPDATES, BLOCK_LEN, D), 1.0, 6.0, ((1, 16),))
    value_rows = noise(streams_of[1], (UPDATES, BLOCK_LEN, D), 1.0, 6.0, ((1, 16), (2, 16)))
    queries = noise(streams_of[2], (UPDATES, BLOCK_LEN, D), 1.0, 6.0, ((1, 16),))
    output_cot = noise(streams_of[3], (UPDATES, BLOCK_LEN, D), 0.2, 3.0, ((1, 16),))
    token_rates = jnp.clip(jnp.exp(math.log(0.02) - 2.30258502 * jax.random.uniform(streams_of[4], (UPDATES, BLOCK_LEN), jnp.float32) ** level_of(streams_of[4], (UPDATES, BLOCK_LEN), ((1, 16),), -0.2, 0.2)), 0.002, 0.02)
    w_first = noise(streams_of[5], (UPDATES, D, H), D ** -0.5, 0.125, ((2, 16),))
    w_second = noise(streams_of[6], (UPDATES, D, H), H ** -0.5, 0.0625, ((2, 16),))
    final_first = noise(streams_of[7], (D, H), 4.0, 24.0, ((0, 16), (1, 16)))
    final_second = noise(streams_of[8], (D, H), 4.0, 24.0, ((0, 16), (1, 16)))
    return {"key_rows": key_rows, "value_rows": value_rows, "queries": queries, "output_cot": output_cot, "token_rates": token_rates, "w_first": w_first, "w_second": w_second, "final_first": final_first, "final_second": final_second}


momentum_decay = 0.9


def silu_terms(hidden):
    sig = jax.nn.sigmoid(hidden)
    slope = sig * (1.0 + hidden * (1.0 - sig))
    curve = sig * (1.0 - sig) * (2.0 + hidden * (1.0 - 2.0 * sig))
    return hidden * sig, slope, curve


def local_backward(keyb, valueb, queryb, cotb, rateb, inner, outer, panel_first, panel_second):
    rate_column = (rateb / BLOCK_LEN)[:, None]
    pre = jnp.dot(keyb, inner, preferred_element_type=jnp.float32)
    act, slope, curve = silu_terms(pre)
    act_b = act.astype(jnp.bfloat16)
    predicted = jnp.dot(act_b, outer.T, preferred_element_type=jnp.float32)
    weighted = (rate_column * (predicted - valueb.astype(jnp.float32))).astype(jnp.bfloat16)
    gated = jnp.dot(weighted, outer, preferred_element_type=jnp.float32)
    delta_b = (gated * slope).astype(jnp.bfloat16)
    query_pre = jnp.dot(queryb, inner, preferred_element_type=jnp.float32)
    read, query_slope, unused = silu_terms(query_pre)
    read_b = read.astype(jnp.bfloat16)
    back_delta = jnp.dot(keyb, panel_first, preferred_element_type=jnp.float32)
    back_gated = (back_delta * slope).astype(jnp.bfloat16)
    back_weighted = jnp.dot(act_b, panel_second.T, preferred_element_type=jnp.float32)
    back_weighted = back_weighted + jnp.dot(back_gated, outer.T, preferred_element_type=jnp.float32)
    back_error = rate_column * back_weighted
    grad_value = (-back_error).astype(jnp.bfloat16)
    back_out = back_error.astype(jnp.bfloat16)
    back_act = jnp.dot(weighted, panel_second, preferred_element_type=jnp.float32)
    back_act = back_act + jnp.dot(back_out, outer, preferred_element_type=jnp.float32)
    back_pre = (back_act * slope + back_delta * gated * curve).astype(jnp.bfloat16)
    back_read = (jnp.dot(cotb, outer, preferred_element_type=jnp.float32) * query_slope).astype(jnp.bfloat16)
    grad_key = jnp.dot(delta_b, panel_first.T, preferred_element_type=jnp.float32)
    grad_key = (grad_key + jnp.dot(back_pre, inner.T, preferred_element_type=jnp.float32)).astype(jnp.bfloat16)
    grad_query = jnp.dot(back_read, inner.T, preferred_element_type=jnp.float32).astype(jnp.bfloat16)
    left_first = jnp.concatenate([keyb, queryb], axis=0)
    right_first = jnp.concatenate([back_pre, back_read], axis=0)
    term_first = jnp.dot(left_first.T, right_first, preferred_element_type=jnp.float32)
    left_second = jnp.concatenate([back_out, weighted, cotb], axis=0)
    right_second = jnp.concatenate([act_b, back_gated, read_b], axis=0)
    term_second = jnp.dot(left_second.T, right_second, preferred_element_type=jnp.float32)
    return grad_key, grad_value, grad_query, term_first, term_second


def reference(key_rows, value_rows, queries, output_cot, token_rates, w_first, w_second, final_first, final_second):
    carry_first = final_first.astype(jnp.float32)
    carry_second = final_second.astype(jnp.float32)
    moment_first = carry_first
    moment_second = carry_second
    key_list = [None] * UPDATES
    value_list = [None] * UPDATES
    query_list = [None] * UPDATES
    for step_index in reversed(range(UPDATES)):
        if step_index < UPDATES - 1:
            moment_first = carry_first + momentum_decay * moment_first
            moment_second = carry_second + momentum_decay * moment_second
        panel_first = (-moment_first).astype(jnp.bfloat16)
        panel_second = (-moment_second).astype(jnp.bfloat16)
        inner = w_first[step_index]
        outer = w_second[step_index]

        def group_step(totals, rows):
            keyb, valueb, queryb, cotb, rateb = rows
            grad_key, grad_value, grad_query, term_first, term_second = local_backward(
                keyb, valueb, queryb, cotb, rateb, inner, outer, panel_first, panel_second)
            new_totals = (totals[0] + term_first, totals[1] + term_second)
            return new_totals, (grad_key, grad_value, grad_query)

        grouped = (key_rows[step_index].reshape(N_TOK, ROWS, D),
                   value_rows[step_index].reshape(N_TOK, ROWS, D),
                   queries[step_index].reshape(N_TOK, ROWS, D),
                   output_cot[step_index].reshape(N_TOK, ROWS, D),
                   token_rates[step_index].reshape(N_TOK, ROWS))
        zeros_start = (jnp.zeros((D, H), jnp.float32), jnp.zeros((D, H), jnp.float32))
        totals, stacked = lax.scan(group_step, zeros_start, grouped)
        carry_first = carry_first + totals[0]
        carry_second = carry_second + totals[1]
        key_list[step_index] = stacked[0].reshape(BLOCK_LEN, D)
        value_list[step_index] = stacked[1].reshape(BLOCK_LEN, D)
        query_list[step_index] = stacked[2].reshape(BLOCK_LEN, D)
    return (jnp.stack(key_list), jnp.stack(value_list), jnp.stack(query_list), carry_first, carry_second)
```

```python
import jax
import jax.numpy as jnp
from jax import lax
from jax.sharding import Mesh, PartitionSpec as P

momentum_decay = 0.9
F32 = jnp.float32
BF16 = jnp.bfloat16

FEAT = ("y", "xh", "core")
TOK = ("xl", "z")
PLANE = FEAT + ("xl",)


def silu_terms(hidden):
    sig = jax.nn.sigmoid(hidden)
    slope = sig * (1.0 + hidden * (1.0 - sig))
    curve = sig * (1.0 - sig) * (2.0 + hidden * (1.0 - 2.0 * sig))
    return (hidden * sig, slope, curve)


def mm(a, b):
    return jnp.dot(a, b, preferred_element_type=F32)


def mm_t(a, b):
    return lax.dot_general(a, b, (((1,), (1,)), ((), ())), preferred_element_type=F32)


def t_mm(a, b):
    return lax.dot_general(a, b, (((0,), (0,)), ((), ())), preferred_element_type=F32)


def swap(x, axis):
    return lax.ppermute(x, axis, [(0, 1), (1, 0)])


def in_order(index, mine, other, axis):
    first = jnp.where(index == 0, mine, other)
    second = jnp.where(index == 0, other, mine)
    return jnp.concatenate([first, second], axis=axis)


def with_partner(rows):
    core = lax.axis_index("core")
    xl = lax.axis_index("xl")
    quarter = rows.shape[2] // 4
    to_right = lax.dynamic_slice_in_dim(rows, core * (2 * quarter), quarter, 2)
    to_left = lax.dynamic_slice_in_dim(rows, core * (2 * quarter) + quarter, quarter, 2)
    x_chips = lax.axis_size("xh") * 2
    from_left = lax.ppermute(to_right, ("xh", "xl"), [(i, (i + 1) % x_chips) for i in range(x_chips)])
    from_right = lax.ppermute(to_left, ("xh", "xl"), [(i, (i - 1) % x_chips) for i in range(x_chips)])
    half = jnp.concatenate([from_left, from_right], axis=2)
    partner = in_order(core, half, swap(half, "core"), 2)
    return in_order(xl, rows, partner, 1)


def plane_scatter(partials, share):
    count = len(partials)
    tokens, width = partials[0].shape
    chunks = jnp.stack([partial.astype(BF16) for partial in partials])
    chunks = chunks.reshape(count, 2, tokens // 2, width // share, share).transpose(3, 1, 0, 2, 4)
    chunks = chunks.reshape(-1, count, tokens // 2, share)
    got = lax.all_to_all(chunks, PLANE, 0, 0, tiled=True)
    sums = jnp.sum(got.astype(F32), axis=0)
    return [sums[i] for i in range(count)]


def plane_gather(part):
    tokens, share = part.shape
    n = lax.axis_size(PLANE)
    got = lax.all_to_all(jnp.broadcast_to(part, (n, tokens, share)), PLANE, 0, 0, tiled=True)
    got = got.reshape(n // 2, 2, tokens, share).transpose(1, 2, 0, 3)
    return got.reshape(2 * tokens, (n // 2) * share)


def on_device(
    key_rows,
    value_rows,
    queries,
    output_cot,
    token_rates,
    w_first,
    w_second,
    final_first,
    final_second,
):
    updates, own_tokens, d_width = key_rows.shape
    share = value_rows.shape[2]
    half = w_first.shape[2] // 2
    slice_rows = final_first.shape[0]
    n_z = lax.axis_size("z")
    block_tokens = own_tokens * n_z * 2
    xl = lax.axis_index("xl")
    last = updates - 1

    def half_of(array, which):
        return lax.dynamic_slice_in_dim(array, which * half, half, array.ndim - 1)

    def both_halves(which):
        return jnp.concatenate([half_of(final_first, which), half_of(final_second, which)], axis=1)

    own_final = both_halves(xl)
    other_final = swap(both_halves(1 - xl), "xl")
    start = in_order(xl, own_final[None], other_final[None], 0)

    def gather_panels(panel):
        full = lax.all_gather(panel, "z", axis=0, tiled=False)
        full = full.transpose(1, 0, 2, 3).reshape(d_width, 2 * half)
        return full[:, :half], full[:, half:]

    inner = half_of(w_first, xl)
    outer = half_of(w_second, xl)
    rate_column = [(token_rates[u] / block_tokens)[:, None] for u in range(updates)]

    def forward(u, key):
        pre = mm(key, inner[u])
        act, slope, curve = silu_terms(pre)
        act_b = act.astype(BF16)
        error = plane_scatter([mm_t(act_b, outer[u])], share)[0] - value_rows[u].astype(F32)
        weighted_part = (rate_column[u] * error).astype(BF16)
        weighted = plane_gather(weighted_part)
        gated = mm(weighted, outer[u])
        delta_b = (gated * slope).astype(BF16)
        return act_b, slope, curve, weighted, gated, delta_b

    def read_out(u, read_rows, cot):
        query_pre = mm(read_rows, inner[u])
        read, query_slope, unused = silu_terms(query_pre)
        back_read = (mm(cot, outer[u]) * query_slope).astype(BF16)
        return read.astype(BF16), back_read

    panels = gather_panels(-start)
    keys = [None] * updates
    keys[last] = with_partner(key_rows[last:])[0]
    rest = jnp.concatenate([key_rows[:last], queries, output_cot], axis=0)
    rest = with_partner(rest)
    for u in range(last):
        keys[u] = rest[u]
    reads = [rest[last + u] for u in range(updates)]
    cots = [rest[last + updates + u] for u in range(updates)]

    carry = start.astype(F32)
    moment = carry
    key_list = [None] * updates
    value_list = [None] * updates
    query_list = [None] * updates
    hidden_sums = []
    early = forward(last, keys[last])
    for u in reversed(range(updates)):
        if u < last:
            moment = carry + momentum_decay * moment
            panels = gather_panels((-moment).astype(BF16))
        panel_first, panel_second = panels
        act_b, slope, curve, weighted, gated, delta_b = early
        read_b, back_read = read_out(u, reads[u], cots[u])
        back_delta = mm(keys[u], panel_first)
        back_gated = (back_delta * slope).astype(BF16)
        back_sum = plane_scatter(
            [mm_t(act_b, panel_second) + mm_t(back_gated, outer[u])], share
        )[0]
        back_error = rate_column[u] * back_sum
        value_list[u] = (-back_error).astype(BF16)
        back_out = plane_gather(back_error.astype(BF16))
        back_act = mm(weighted, panel_second) + mm(back_out, outer[u])
        back_pre = (back_act * slope + back_delta * gated * curve).astype(BF16)
        term_first = t_mm(keys[u], back_pre) + t_mm(reads[u], back_read)
        term_second = t_mm(back_out, act_b) + t_mm(weighted, back_gated) + t_mm(cots[u], read_b)
        terms = jnp.concatenate([term_first, term_second], axis=1).astype(BF16)
        terms = terms.reshape(2, n_z, slice_rows, 2 * half).transpose(1, 0, 2, 3)
        terms = terms.reshape(d_width, 2 * half)
        hidden_sums.append((key_list, u, (delta_b, panel_first, back_pre, inner[u])))
        hidden_sums.append((query_list, u, (back_read, inner[u])))
        if u > 0:
            terms, keys[u - 1] = lax.optimization_barrier((terms, keys[u - 1]))
            early = forward(u - 1, keys[u - 1])
        else:
            partials = []
            for unused, unused_u, factors in hidden_sums:
                pairs = list(zip(factors[::2], factors[1::2]))
                partials.append(sum(mm_t(left, right) for left, right in pairs))
            sums = plane_scatter(partials, share)
            for (where, at, unused), total in zip(hidden_sums, sums):
                where[at] = total.astype(BF16)
        total = lax.psum_scatter(terms, "z", scatter_dimension=0, tiled=True)
        carry = carry + total.astype(F32).reshape(carry.shape)

    kept = lax.dynamic_index_in_dim(carry, xl, 0, keepdims=False)
    sent = swap(lax.dynamic_index_in_dim(carry, 1 - xl, 0, keepdims=False), "xl")
    grad_first = in_order(xl, kept[:, :half], sent[:, :half], 1)
    grad_second = in_order(xl, kept[:, half:], sent[:, half:], 1)
    return (
        jnp.stack(key_list),
        jnp.stack(value_list),
        jnp.stack(query_list),
        grad_first,
        grad_second,
    )


def solution(mesh):
    n_feat, n_tok = mesh.devices.shape
    fine = Mesh(
        mesh.devices.reshape(n_feat // 4, 2, 2, 2, n_tok // 2), ("y", "xh", "core", "xl", "z")
    )
    return jax.shard_map(
        on_device,
        mesh=fine,
        in_specs=(
            P(None, TOK, None),
            P(None, TOK, FEAT),
            P(None, TOK, None),
            P(None, TOK, None),
            P(None, TOK),
            P(None, None, FEAT),
            P(None, None, FEAT),
            P(TOK, FEAT),
            P(TOK, FEAT),
        ),
        out_specs=(
            P(None, TOK, FEAT),
            P(None, TOK, FEAT),
            P(None, TOK, FEAT),
            P(TOK, FEAT),
            P(TOK, FEAT),
        ),
        check_vma=False,
    )
```

```python
import jax
import jax.numpy as jnp
from jax import lax
from jax.sharding import Mesh, PartitionSpec as P

momentum_decay = 0.9
F32 = jnp.float32
BF16 = jnp.bfloat16

FEAT = ("y", "xh", "core")
TOK = ("xl", "z")
PLANE = FEAT + ("xl",)


def silu_terms(hidden):
    sig = jax.nn.sigmoid(hidden)
    slope = sig * (1.0 + hidden * (1.0 - sig))
    curve = sig * (1.0 - sig) * (2.0 + hidden * (1.0 - 2.0 * sig))
    return (hidden * sig, slope, curve)


def mm(a, b):
    return jnp.dot(a, b, preferred_element_type=F32)


def mm_t(a, b):
    return lax.dot_general(a, b, (((1,), (1,)), ((), ())), preferred_element_type=F32)


def t_mm(a, b):
    return lax.dot_general(a, b, (((0,), (0,)), ((), ())), preferred_element_type=F32)


def swap(x, axis):
    return lax.ppermute(x, axis, [(0, 1), (1, 0)])


def in_order(index, mine, other, axis):
    first = jnp.where(index == 0, mine, other)
    second = jnp.where(index == 0, other, mine)
    return jnp.concatenate([first, second], axis=axis)


def with_partner(rows):
    core = lax.axis_index("core")
    xl = lax.axis_index("xl")
    quarter = rows.shape[2] // 4
    to_right = lax.dynamic_slice_in_dim(rows, core * (2 * quarter), quarter, 2)
    to_left = lax.dynamic_slice_in_dim(rows, core * (2 * quarter) + quarter, quarter, 2)
    x_chips = lax.axis_size("xh") * 2
    from_left = lax.ppermute(to_right, ("xh", "xl"), [(i, (i + 1) % x_chips) for i in range(x_chips)])
    from_right = lax.ppermute(to_left, ("xh", "xl"), [(i, (i - 1) % x_chips) for i in range(x_chips)])
    half = jnp.concatenate([from_left, from_right], axis=2)
    partner = in_order(core, half, swap(half, "core"), 2)
    return in_order(xl, rows, partner, 1)


def scatter_chunks(partial, share):
    tokens, width = partial.shape
    chunks = partial.astype(BF16).reshape(2, tokens // 2, width // share, share)
    return chunks.transpose(2, 0, 1, 3).reshape(-1, tokens // 2, share)


def gather_chunks(part):
    return jnp.broadcast_to(part, (lax.axis_size(PLANE),) + part.shape)


def exchange(chunk_list):
    got = lax.all_to_all(jnp.stack(chunk_list, axis=1), PLANE, 0, 0, tiled=True)
    return [got[:, i] for i in range(len(chunk_list))]


def summed(got):
    return jnp.sum(got.astype(F32), axis=0)


def joined(got):
    n, tokens, share = got.shape
    got = got.reshape(n // 2, 2, tokens, share).transpose(1, 2, 0, 3)
    return got.reshape(2 * tokens, (n // 2) * share)


def on_device(
    key_rows,
    value_rows,
    queries,
    output_cot,
    token_rates,
    w_first,
    w_second,
    final_first,
    final_second,
):
    updates, own_tokens, d_width = key_rows.shape
    share = value_rows.shape[2]
    half = w_first.shape[2] // 2
    slice_rows = final_first.shape[0]
    n_z = lax.axis_size("z")
    block_tokens = own_tokens * n_z * 2
    xl = lax.axis_index("xl")
    last = updates - 1

    def half_of(array, which):
        return lax.dynamic_slice_in_dim(array, which * half, half, array.ndim - 1)

    def both_halves(which):
        return jnp.concatenate([half_of(final_first, which), half_of(final_second, which)], axis=1)

    own_final = both_halves(xl)
    other_final = swap(both_halves(1 - xl), "xl")
    start = in_order(xl, own_final[None], other_final[None], 0)

    def gather_panels(panel):
        full = lax.all_gather(panel, "z", axis=0, tiled=False)
        full = full.transpose(1, 0, 2, 3).reshape(d_width, 2 * half)
        return full[:, :half], full[:, half:]

    inner = half_of(w_first, xl)
    outer = half_of(w_second, xl)
    rate_column = [(token_rates[u] / block_tokens)[:, None] for u in range(updates)]

    panels = gather_panels(-start)
    keys = [None] * updates
    keys[last] = with_partner(key_rows[last:])[0]
    rest = jnp.concatenate([key_rows[:last], queries, output_cot], axis=0)
    rest = with_partner(rest)
    for u in range(last):
        keys[u] = rest[u]
    reads = [rest[last + u] for u in range(updates)]
    cots = [rest[last + updates + u] for u in range(updates)]

    def forward(u):
        act, slope, curve = silu_terms(mm(keys[u], inner[u]))
        act_b = act.astype(BF16)
        return act_b, slope, curve, scatter_chunks(mm_t(act_b, outer[u]), share)

    def weigh(u, got):
        error = summed(got) - value_rows[u].astype(F32)
        return (rate_column[u] * error).astype(BF16)

    def read_out(u):
        read, query_slope, unused = silu_terms(mm(reads[u], inner[u]))
        back_read = (mm(cots[u], outer[u]) * query_slope).astype(BF16)
        return read.astype(BF16), back_read, scatter_chunks(mm_t(back_read, inner[u]), share)

    carry = start.astype(F32)
    moment = carry
    totals = []
    key_list = [None] * updates
    value_list = [None] * updates
    query_list = [None] * updates
    key_chunks = [None] * updates
    query_chunks = [None] * updates
    weighted = None
    act_b, slope, curve, error_chunks = forward(last)
    weighted_part = weigh(last, exchange([error_chunks])[0])
    for u in reversed(range(updates)):
        panel_first, panel_second = panels
        read_b, back_read, query_chunks[u] = read_out(u)
        back_delta = mm(keys[u], panel_first)
        back_gated = (back_delta * slope).astype(BF16)
        back_sum = mm_t(act_b, panel_second) + mm_t(back_gated, outer[u])
        back_error = rate_column[u] * summed(exchange([scatter_chunks(back_sum, share)])[0])
        value_list[u] = (-back_error).astype(BF16)
        back_part = back_error.astype(BF16)
        if weighted is None:
            got = exchange([gather_chunks(back_part), gather_chunks(weighted_part)])
            back_out, weighted = joined(got[0]), joined(got[1])
        else:
            back_out = joined(exchange([gather_chunks(back_part)])[0])
        gated = mm(weighted, outer[u])
        delta_b = (gated * slope).astype(BF16)
        back_act = mm(weighted, panel_second) + mm(back_out, outer[u])
        back_pre = (back_act * slope + back_delta * gated * curve).astype(BF16)
        term_first = t_mm(keys[u], back_pre) + t_mm(reads[u], back_read)
        term_second = t_mm(back_out, act_b) + t_mm(weighted, back_gated) + t_mm(cots[u], read_b)
        terms = jnp.concatenate([term_first, term_second], axis=1).astype(BF16)
        terms = terms.reshape(2, n_z, slice_rows, 2 * half).transpose(1, 0, 2, 3)
        terms = terms.reshape(d_width, 2 * half)
        if u > 0:
            key_chunks[u] = scatter_chunks(
                mm_t(delta_b, panel_first) + mm_t(back_pre, inner[u]), share
            )
            act_b, slope, curve, error_chunks = forward(u - 1)
            terms, error_chunks, now = lax.optimization_barrier(
                (terms, error_chunks, query_chunks[u])
            )
            got = exchange([error_chunks, now])
            total = lax.psum_scatter(terms, "z", scatter_dimension=0, tiled=True)
            weighted_part = weigh(u - 1, got[0])
            query_list[u] = summed(got[1]).astype(BF16)
            total, weighted_part, query_list[u] = lax.optimization_barrier(
                (total, weighted_part, query_list[u])
            )
            totals.append(total)
            carry = carry + total.astype(F32).reshape(carry.shape)
            moment = carry + momentum_decay * moment
            panel = (-moment).astype(BF16)
            panel, weighted_part = lax.optimization_barrier((panel, weighted_part))
            sent = [gather_chunks(weighted_part)]
            if u == 1:
                query_chunks[0] = read_out(0)[2]
                sent.append(query_chunks[0])
            got = exchange(sent)
            weighted = joined(got[0])
            if u == 1:
                query_list[0] = summed(got[1]).astype(BF16)
            panels = gather_panels(panel)
            panels, weighted = lax.optimization_barrier((panels, weighted))
        else:
            terms, delta_b, back_pre, panel_first = lax.optimization_barrier(
                (terms, delta_b, back_pre, panel_first)
            )
            total = lax.psum_scatter(terms, "z", scatter_dimension=0, tiled=True)
            totals.append(total)
            key_chunks[u] = scatter_chunks(
                mm_t(delta_b, panel_first) + mm_t(back_pre, inner[u]), share
            )
    for u, got in enumerate(exchange(key_chunks)):
        key_list[u] = summed(got).astype(BF16)

    grad_first = final_first.astype(F32)
    grad_second = final_second.astype(F32)
    for total in totals:
        total = total.reshape(carry.shape)
        kept = lax.dynamic_index_in_dim(total, xl, 0, keepdims=False)
        sent = swap(lax.dynamic_index_in_dim(total, 1 - xl, 0, keepdims=False), "xl")
        grad_first = grad_first + in_order(xl, kept[:, :half], sent[:, :half], 1)
        grad_second = grad_second + in_order(xl, kept[:, half:], sent[:, half:], 1)
    return (
        jnp.stack(key_list),
        jnp.stack(value_list),
        jnp.stack(query_list),
        grad_first,
        grad_second,
    )


def solution(mesh):
    n_feat, n_tok = mesh.devices.shape
    fine = Mesh(
        mesh.devices.reshape(n_feat // 4, 2, 2, 2, n_tok // 2), ("y", "xh", "core", "xl", "z")
    )
    return jax.shard_map(
        on_device,
        mesh=fine,
        in_specs=(
            P(None, TOK, None),
            P(None, TOK, FEAT),
            P(None, TOK, None),
            P(None, TOK, None),
            P(None, TOK),
            P(None, None, FEAT),
            P(None, None, FEAT),
            P(TOK, FEAT),
            P(TOK, FEAT),
        ),
        out_specs=(
            P(None, TOK, FEAT),
            P(None, TOK, FEAT),
            P(None, TOK, FEAT),
            P(TOK, FEAT),
            P(TOK, FEAT),
        ),
        check_vma=False,
    )
```

```python
import math

import jax
import jax.numpy as jnp
from jax import lax
from jax.experimental import pallas as pl
from jax.experimental.pallas import tpu as pltpu
from jax.sharding import Mesh, PartitionSpec as P

momentum_decay = 0.9
F32 = jnp.float32
BF16 = jnp.bfloat16

FEAT = ("y", "xh", "core")
TOK = ("xl", "z")
PLANE = FEAT + ("xl",)


def silu_terms(hidden):
    sig = jax.nn.sigmoid(hidden)
    slope = sig * (1.0 + hidden * (1.0 - sig))
    curve = sig * (1.0 - sig) * (2.0 + hidden * (1.0 - 2.0 * sig))
    return (hidden * sig, slope, curve)


def mm(a, b):
    return jnp.dot(a, b, preferred_element_type=F32)


def mm_t(a, b):
    return lax.dot_general(a, b, (((1,), (1,)), ((), ())), preferred_element_type=F32)


def t_mm(a, b):
    return lax.dot_general(a, b, (((0,), (0,)), ((), ())), preferred_element_type=F32)


def swap(x, axis):
    return lax.ppermute(x, axis, [(0, 1), (1, 0)])


def in_order(index, mine, other, axis):
    first = jnp.where(index == 0, mine, other)
    second = jnp.where(index == 0, other, mine)
    return jnp.concatenate([first, second], axis=axis)


def shape(dims, dtype):
    return jax.ShapeDtypeStruct(dims, dtype)


def call(body, name, flops, out_shapes, operands, scratch=()):
    operands = [x if isinstance(x, tuple) else (x, x.shape, None) for x in operands]
    n, m = len(operands), len(out_shapes)
    total = sum(x.size * x.dtype.itemsize for x in [y[0] for y in operands] + list(out_shapes))

    def kernel(*refs):
        sources, targets = refs[:n], refs[n : n + m]
        held, out = refs[n + m : 2 * n + m], refs[2 * n + m : 2 * n + 2 * m]
        in_sems, out_sems = refs[2 * n + 2 * m : 2 * n + 2 * m + 2]
        rest = refs[2 * n + 2 * m + 2 :]
        copies = []
        count = 0
        for i, (unused, unused_dims, pieces) in enumerate(operands):
            copies.append([])
            parts = [(sources[i], None)] if pieces is None else pieces(sources[i])
            for source, at in parts:
                target = held[i] if at is None else held[i].at[at]
                copies[i].append(pltpu.make_async_copy(source, target, in_sems.at[count]))
                copies[i][-1].start()
                count += 1
        here = set()
        sent = []

        def take(i, piece=None):
            for p in range(len(copies[i])) if piece is None else [piece]:
                if (i, p) not in here:
                    copies[i][p].wait()
                    here.add((i, p))
            return held[i]

        def give(i, at=None, source_at=None):
            source = out[i] if at is None else out[i].at[at if source_at is None else source_at]
            target = targets[i] if at is None else targets[i].at[at]
            sent.append(pltpu.make_async_copy(source, target, out_sems.at[len(sent)]))
            sent[-1].start()

        body(take, out, give, *rest)
        for i in range(n):
            take(i)
        for copy in sent:
            copy.wait()

    return pl.pallas_call(
        kernel,
        name=name,
        out_shape=list(out_shapes),
        in_specs=[pl.BlockSpec(memory_space=pltpu.HBM)] * n,
        out_specs=[pl.BlockSpec(memory_space=pltpu.HBM)] * m,
        scratch_shapes=[pltpu.VMEM(dims, x.dtype) for x, dims, unused in operands]
        + [pltpu.VMEM(x.shape, x.dtype) for x in out_shapes]
        + [pltpu.SemaphoreType.DMA((64,)), pltpu.SemaphoreType.DMA((64,))]
        + list(scratch),
        compiler_params=pltpu.CompilerParams(vmem_limit_bytes=64 << 20),
        cost_estimate=pl.CostEstimate(flops=flops, bytes_accessed=total, transcendentals=0),
    )(*[x for x, unused, unused_pieces in operands])


def weight(array, u, n_z):
    rows, half = array.shape[3], array.shape[4] // 2

    def pieces(ref):
        cols = pl.ds(pl.multiple_of(lax.axis_index("xl") * half, half), half)
        return [(ref.at[u, x, :, :, cols], (slice(None), x)) for x in range(2)]

    return array, (n_z, 2, rows, half), pieces


def flat(ref):
    n_z, two, rows, half = ref.shape
    return ref[...].reshape(n_z * two * rows, half)


def flat_block(ref, z):
    return ref[z].reshape(-1, ref.shape[3])


def layer(panels, which):
    n_z, both, block = panels.shape
    half = both // 2
    at = pl.ds(which * half, half)
    part = n_z // 2
    return panels, (n_z, half, block), lambda ref: [
        (ref.at[pl.ds(i * part, part), at], pl.ds(i * part, part)) for i in range(2)
    ]


def slot_of(got, slot):
    n, unused, tokens, share = got.shape
    part = n // 4
    return got, (n, tokens, share), lambda ref: [
        (ref.at[pl.ds(i * part, part), slot], pl.ds(i * part, part)) for i in range(4)
    ]


def row_of(array, u):
    return array, array.shape[1:], lambda ref: [(ref.at[u], None)]


def lay_out(part, chunks, slot, z):
    n_z = chunks.shape[0] // 4
    tokens, share = part.shape[0] // 2, part.shape[1] // 2
    for x in range(2):
        for t in range(2):
            chunks[(x * n_z + z) * 2 + t, slot] = part[
                t * tokens : (t + 1) * tokens, x * share : (x + 1) * share
            ]


def sent_rows(z, n_z):
    return [pl.ds((x * n_z + z - 1) * 2, 4) for x in range(2)] if z % 2 else []


def lay_in(take, i, rows):
    got = take(i, 0)
    n_z = got.shape[0] // 4
    tokens, share = got.shape[1:]
    for x in range(2):
        for z in range(n_z):
            for t in range(2):
                chunk = (x * n_z + z) * 2 + t
                take(i, chunk // n_z)
                at = (2 * z + x) * share
                rows[t * tokens : (t + 1) * tokens, at : at + share] = got[chunk]


def errors(key_rows, w_first, w_second, share):
    updates, tokens, width = key_rows.shape
    full = w_first.shape[2]
    dims = (width // share, updates, tokens, share)

    def body(take, out, give):
        chunks = out[0]
        for u in reversed(range(updates)):
            rows = take(0)[u]
            pre = mm(rows, take(1, updates - 1 - u)[u])
            act = (pre * jax.nn.sigmoid(pre)).astype(BF16)
            predicted = mm_t(act, take(2, updates - 1 - u)[u]).astype(BF16)
            for f in range(dims[0]):
                chunks[f, u] = predicted[:, f * share : (f + 1) * share]
        for f in range(0, dims[0], 4):
            give(0, pl.ds(f, 4))

    def by_update(array):
        order = reversed(range(updates))
        return array, array.shape, lambda ref: [(ref.at[u], u) for u in order]

    return call(
        body,
        "errors",
        4 * key_rows.size * full,
        [shape(dims, BF16)],
        [key_rows, by_update(w_first), by_update(w_second)],
    )[0]


def weigh_out(got, values, rates, plane):
    n, updates, tokens, share = got.shape

    def body(take, out, give):
        parts, spread_out = out
        terms, value, rate = take(0), take(1), take(2)
        for u in reversed(range(updates)):
            total = terms[0, u].astype(F32)
            for i in range(1, n):
                total += terms[i, u].astype(F32)
            rounded = (rate[u] * (total - value[u].astype(F32))).astype(BF16)
            parts[u] = rounded
            if u == updates - 1:
                for i in range(8):
                    spread_out[i, 0] = rounded
                for i in range(0, plane, 8):
                    give(1, pl.ds(i, 8), pl.ds(0, 8))
        give(0)

    return call(
        body,
        "weigh_out",
        got.size,
        [shape(values.shape, BF16), shape((plane, 1, tokens, share), BF16)],
        [got, values, rates],
    )


def assemble(rows, from_left, from_right, swapped, n_z):
    n, tokens, width = rows.shape
    share = width // (2 * n_z)
    quarter, half = from_left.shape[2], swapped.shape[2]

    def body(take, out, give):
        full = out[0]
        core = lax.axis_index("core")
        xl = lax.axis_index("xl")
        mine = pl.ds(pl.multiple_of(xl * tokens, tokens), tokens)
        other = pl.ds(pl.multiple_of((1 - xl) * tokens, tokens), tokens)
        for i in range(n):
            for x in range(2):
                for z in range(n_z):
                    at = (2 * z + x) * share
                    block = x * half + z * share
                    full[i, mine, at : at + share] = take(0)[i, :, block : block + share]
            for z in range(n_z):
                at = z * share
                if at < quarter:
                    piece = take(1)[i, :, at : at + share]
                else:
                    piece = take(2)[i, :, at - quarter : at - quarter + share]
                place = pl.multiple_of((2 * z + core) * share, share)
                full[i, other, pl.ds(place, share)] = piece
                place = pl.multiple_of((2 * z + 1 - core) * share, share)
                full[i, other, pl.ds(place, share)] = take(3)[i, :, at : at + share]
            give(0, i)

    return call(
        body,
        "assemble",
        rows.size,
        [shape((n, 2 * tokens, width), BF16)],
        [rows, from_left, from_right, swapped],
    )[0]


def from_partner(rows):
    core = lax.axis_index("core")
    quarter = rows.shape[2] // 4
    to_right = lax.dynamic_slice_in_dim(rows, core * (2 * quarter), quarter, 2)
    to_left = lax.dynamic_slice_in_dim(rows, core * (2 * quarter) + quarter, quarter, 2)
    x_chips = lax.axis_size("xh") * 2
    from_left = lax.ppermute(to_right, ("xh", "xl"), [(i, (i + 1) % x_chips) for i in range(x_chips)])
    from_right = lax.ppermute(to_left, ("xh", "xl"), [(i, (i - 1) % x_chips) for i in range(x_chips)])
    return rows, from_left, from_right


def whole(pieces, n_z):
    rows, from_left, from_right = pieces
    swapped = swap(jnp.concatenate([from_left, from_right], axis=2), "core")
    return assemble(rows, from_left, from_right, swapped, n_z)


def forward(keys, inner, u):
    tokens = keys.shape[1]
    half = inner.shape[4] // 2
    n_z = inner.shape[2]

    def body(take, out, give):
        act, slope, curve = silu_terms(mm(take(0)[...], flat(take(1))))
        for i, value in enumerate([act.astype(BF16), act.T.astype(BF16), slope, curve]):
            out[i][...] = value
            give(i)

    hidden = (tokens, half)
    return call(
        body,
        "forward",
        2 * keys[u].size * half,
        [shape(hidden, BF16), shape((half, tokens), BF16), shape(hidden, F32), shape(hidden, F32)],
        [row_of(keys, u), weight(inner, u, n_z)],
    )


def read_out(reads, cots, inner, outer, u):
    tokens = reads.shape[1]
    half = inner.shape[4] // 2
    n_z = inner.shape[2]

    def body(take, out, give):
        read, slope, unused = silu_terms(mm(take(0)[...], flat(take(2))))
        back_read = mm(take(1)[...], flat(take(3))) * slope
        values = [read.T.astype(BF16), back_read.astype(BF16), back_read.T.astype(BF16)]
        for i, value in enumerate(values):
            out[i][...] = value
            give(i)

    turned = shape((half, tokens), BF16)
    return call(
        body,
        "read_out",
        4 * reads[u].size * half,
        [turned, shape((tokens, half), BF16), turned],
        [row_of(reads, u), row_of(cots, u), weight(inner, u, n_z), weight(outer, u, n_z)],
    )


def weigh_in(got, outer, slope, u):
    n_z = outer.shape[2]
    tokens, half = slope.shape
    width = 2 * n_z * outer.shape[3]

    def body(take, out, give):
        rows, gated, delta = out
        lay_in(take, 0, rows)
        give(0)
        total = mm(rows[...], flat(take(1)))
        gated[...] = total
        give(1)
        delta[...] = (total * take(2)[...]).astype(BF16)
        give(2)

    return call(
        body,
        "weigh_in",
        2 * tokens * width * half,
        [shape((tokens, width), BF16), shape((tokens, half), F32), shape((tokens, half), BF16)],
        [slot_of(got, 0), weight(outer, u, n_z), slope],
    )


def back(panels, keys, slope, act, outer, chunk_shape, u):
    n_z, both, block = panels.shape
    half = both // 2
    tokens = slope.shape[0]

    def body(take, out, give):
        back_delta, back_gated, back_gated_t, chunks = out
        rows = take(0)
        total = jnp.zeros((tokens, half), F32)
        for z in range(n_z):
            total += mm_t(rows[:, z * block : (z + 1) * block], take(1, 2 * z // n_z)[z])
        back_delta[...] = total
        give(0)
        gated = total * take(2)[...]
        gated_b = gated.astype(BF16)
        back_gated[...] = gated_b
        give(1)
        act_in, outer_in = take(3)[...], take(4)
        for z in range(n_z):
            part = mm(act_in, take(5, 2 * z // n_z)[z]) + mm_t(gated_b, flat_block(outer_in, z))
            lay_out(part.astype(BF16), chunks, 0, z)
            for rows_out in sent_rows(z, n_z):
                give(3, rows_out)
        back_gated_t[...] = gated.T.astype(BF16)
        give(2)

    hidden = (tokens, half)
    return call(
        body,
        "back",
        6 * keys[u].size * half,
        [shape(hidden, F32), shape(hidden, BF16), shape((half, tokens), BF16), shape(chunk_shape, BF16)],
        [row_of(keys, u), layer(panels, 0), slope, act, weight(outer, u, n_z), layer(panels, 1)],
    )


def sum_error(got, rates, u):
    n, unused, tokens, share = got.shape

    def body(take, out, give):
        part, spread_out = out
        total = jnp.zeros((tokens, share), F32)
        for i in range(n):
            total += take(0, i * 4 // n)[i].astype(F32)
        rounded = (take(1)[...] * total).astype(BF16)
        part[...] = rounded
        give(0)
        for i in range(8):
            spread_out[i, 0] = rounded
        for i in range(0, n, 8):
            give(1, pl.ds(i, 8), pl.ds(0, 8))

    return call(
        body,
        "error",
        n * tokens * share,
        [shape((tokens, share), BF16), shape(got.shape, BF16)],
        [slot_of(got, 0), row_of(rates, u)],
    )


def base_of(panels, weighted, slope, curve, back_delta, gated):
    n_z, both, block = panels.shape

    def body(take, out, give):
        rows = take(0)
        total = jnp.zeros(slope.shape, F32)
        for z in range(n_z):
            total += mm_t(rows[:, z * block : (z + 1) * block], take(1, 2 * z // n_z)[z])
        out[0][...] = total * take(2)[...] + take(3)[...] * take(4)[...] * take(5)[...]
        give(0)

    return call(
        body,
        "base",
        weighted.size * both,
        [shape(slope.shape, F32)],
        [weighted, layer(panels, 1), slope, curve, back_delta, gated],
    )[0]


def terms_of(got, base, slope, outer, keys, weighted, reads, cots, factors, u):
    tokens, half = slope.shape
    n_z = outer.shape[2]
    width = keys.shape[2]
    block = width // n_z

    def body(take, out, give, back_out):
        back_pre, terms = out
        lay_in(take, 0, back_out)
        pre = take(3)[...] + mm(back_out[...], flat(take(1))) * take(2)[...]
        back_pre[...] = pre.astype(BF16)
        give(0)
        pre_t = pre.T.astype(BF16)
        act_t, back_gated_t, read_t, back_read_t = [take(4 + i)[...] for i in range(4)]
        key, rows, read_rows, cot = [take(8 + i) for i in range(4)]
        for z in range(n_z):
            cols = slice(z * block, (z + 1) * block)
            first = mm(pre_t, key[:, cols]) + mm(back_read_t, read_rows[:, cols])
            terms[z, :half, :] = first.astype(BF16)
            second = mm(act_t, back_out[:, cols]) + mm(back_gated_t, rows[:, cols])
            second += mm(read_t, cot[:, cols])
            terms[z, half:, :] = second.astype(BF16)
            give(1, z)

    return call(
        body,
        "terms",
        12 * tokens * width * half,
        [shape((tokens, half), BF16), shape((n_z, 2 * half, block), BF16)],
        [slot_of(got, 0), weight(outer, u, n_z), slope, base]
        + list(factors)
        + [row_of(keys, u), weighted, row_of(reads, u), row_of(cots, u)],
        scratch=[pltpu.VMEM((tokens, width), BF16)],
    )


def spread(parts, n_z, share):
    operands = []
    for part in parts:
        if isinstance(part, list):
            for pair in part:
                operands.extend(pair)
        else:
            operands.append(part)
    tokens = share
    dims = (4 * n_z, len(parts), tokens, share)

    def body(take, out, give):
        chunks = out[0]
        for z in range(n_z):
            at = 0
            for slot, part in enumerate(parts):
                if not isinstance(part, list):
                    for x in range(2):
                        for t in range(2):
                            chunks[(x * n_z + z) * 2 + t, slot] = take(at)[...]
                    at += 1
                    continue
                total = None
                for rows, operand in part:
                    if len(operand[1]) == 3:
                        term = mm(take(at)[...], take(at + 1, 2 * z // n_z)[z])
                    else:
                        term = mm_t(take(at)[...], flat_block(take(at + 1), z))
                    total = term if total is None else total + term
                    at += 2
                lay_out(total.astype(BF16), chunks, slot, z)
            for rows_out in sent_rows(z, n_z):
                give(0, rows_out)

    flops = sum(4 * tokens * math.prod(x[1]) for x in operands if isinstance(x, tuple))
    return call(body, "spread", flops, [shape(dims, BF16)], operands)[0]


def exchange(chunks):
    return lax.all_to_all(chunks, PLANE, 0, 0, tiled=True)


def summed(got, slot):
    return jnp.sum(got[:, slot].astype(F32), axis=0)


def after(value, other):
    return lax.optimization_barrier((value, other))[0]


def on_device(
    key_rows,
    value_rows,
    queries,
    output_cot,
    token_rates,
    w_first,
    w_second,
    final_first,
    final_second,
):
    updates, own_tokens, d_width = key_rows.shape
    share = value_rows.shape[2]
    half = w_first.shape[2] // 2
    n_z = lax.axis_size("z")
    block_tokens = 2 * own_tokens * n_z
    xl = lax.axis_index("xl")
    last = updates - 1
    plane = lax.axis_size(PLANE)

    def both_halves(which):
        parts = [
            lax.dynamic_slice_in_dim(array, which * half, half, 1)
            for array in (final_first, final_second)
        ]
        return jnp.concatenate(parts, axis=1)

    other_final = swap(both_halves(1 - xl), "xl")
    start = in_order(xl, both_halves(xl), other_final, 0).T
    panels = lax.all_gather(-start, "z", axis=0, tiled=False)

    rates = jnp.broadcast_to((token_rates / block_tokens)[:, :, None], value_rows.shape)
    inner = w_first.reshape(updates, 2, n_z, -1, 2 * half)
    outer = w_second.reshape(updates, 2, n_z, -1, 2 * half)

    key_pieces = from_partner(key_rows)
    error_chunks = after(errors(key_rows, w_first, w_second, share), (start, key_pieces))
    got = lax.all_to_all(error_chunks, FEAT, 0, 0, tiled=True)
    read_pieces = from_partner(after(queries, error_chunks))
    cot_pieces = from_partner(after(output_cot, error_chunks))
    keys = whole(key_pieces, n_z)
    hidden = [None] * updates
    hidden[last] = forward(keys, inner, last)
    got = after(got, (hidden[last], read_pieces, cot_pieces))
    weighted_part, chunks = weigh_out(got, value_rows, rates, plane)
    got = exchange(chunks)
    reads = whole(read_pieces, n_z)
    cots = whole(cot_pieces, n_z)
    read_list = [None] * updates
    read_list[last] = read_out(reads, cots, inner, outer, last)
    panels, got, reads, cots, read_list[last] = lax.optimization_barrier(
        (panels, got, reads, cots, read_list[last])
    )

    next_in = weigh_in(got, outer, hidden[last][2], last)
    carry = start.astype(F32)
    moment = carry
    totals = []
    key_list = [None] * updates
    value_list = [None] * updates
    query_list = [None] * updates
    for u in reversed(range(updates)):
        act, act_t, slope, curve = hidden[u]
        read_t, back_read, back_read_t = read_list[u]
        weighted, gated, delta = next_in
        back_delta, back_gated, back_gated_t, chunks = back(
            panels, keys, slope, act, outer, (plane, 1, own_tokens, share), u
        )
        base = base_of(panels, weighted, slope, curve, back_delta, gated)
        got = after(exchange(chunks), base)
        if u > 0:
            chunks_now = spread(
                [
                    (weighted_part, (own_tokens, share), lambda ref: [(ref.at[u - 1], None)]),
                    [(back_read, weight(inner, u, n_z))],
                ],
                n_z,
                share,
            )
            got = after(got, chunks_now)
        back_part, chunks = sum_error(got, rates, u)
        value_list[u] = -back_part
        got = exchange(chunks)
        if u > 0:
            hidden[u - 1] = forward(keys, inner, u - 1)
            read_list[u - 1] = read_out(reads, cots, inner, outer, u - 1)
            got = after(got, (hidden[u - 1], read_list[u - 1]))
        back_pre, terms = terms_of(
            got,
            base,
            slope,
            outer,
            keys,
            weighted,
            reads,
            cots,
            [act_t, back_gated_t, read_t, back_read_t],
            u,
        )
        key_parts = [(delta, layer(panels, 0)), (back_pre, weight(inner, u, n_z))]
        total = lax.psum_scatter(terms, "z", scatter_dimension=0, tiled=True)[0]
        totals.append(total)
        if u > 0:
            got = exchange(after(chunks_now, terms))
            parts = [key_parts]
            if u == 1:
                parts.append([(read_list[0][1], weight(inner, 0, n_z))])
            chunks = spread(parts, n_z, share)
            total, got, chunks = lax.optimization_barrier((total, got, chunks))
            carry = carry + total.astype(F32)
            moment = carry + momentum_decay * moment
            panel = (-moment).astype(BF16)
            panels = lax.all_gather(panel, "z", axis=0, tiled=False)
            sums = exchange(after(chunks, panel))
            query_list[u] = summed(after(got, panel), 1).astype(BF16)
            next_in = weigh_in(after(got, panel), outer, hidden[u - 1][2], u - 1)
            panels, sums, next_in = lax.optimization_barrier((panels, sums, next_in))
            key_list[u] = summed(sums, 0).astype(BF16)
            if u == 1:
                query_list[0] = summed(sums, 1).astype(BF16)
        else:
            key_list[u] = summed(exchange(spread([key_parts], n_z, share)), 0).astype(BF16)

    grad_first = final_first.astype(F32)
    grad_second = final_second.astype(F32)
    for total in totals:
        total = total.reshape(2 * half, 2, -1)
        kept = lax.dynamic_index_in_dim(total, xl, 1, keepdims=False).T
        sent = swap(lax.dynamic_index_in_dim(total, 1 - xl, 1, keepdims=False), "xl").T
        grad_first = grad_first + in_order(xl, kept[:, :half], sent[:, :half], 1)
        grad_second = grad_second + in_order(xl, kept[:, half:], sent[:, half:], 1)
    return (
        jnp.stack(key_list),
        jnp.stack(value_list),
        jnp.stack(query_list),
        grad_first,
        grad_second,
    )


def solution(mesh):
    n_feat, n_tok = mesh.devices.shape
    fine = Mesh(
        mesh.devices.reshape(n_feat // 4, 2, 2, 2, n_tok // 2), ("y", "xh", "core", "xl", "z")
    )
    return jax.shard_map(
        on_device,
        mesh=fine,
        in_specs=(
            P(None, TOK, None),
            P(None, TOK, FEAT),
            P(None, TOK, None),
            P(None, TOK, None),
            P(None, TOK),
            P(None, None, FEAT),
            P(None, None, FEAT),
            P(TOK, FEAT),
            P(TOK, FEAT),
        ),
        out_specs=(
            P(None, TOK, FEAT),
            P(None, TOK, FEAT),
            P(None, TOK, FEAT),
            P(TOK, FEAT),
            P(TOK, FEAT),
        ),
        check_vma=False,
    )
```

```python
import math

import jax
import jax.numpy as jnp
from jax import lax
from jax.experimental import pallas as pl
from jax.experimental.pallas import tpu as pltpu
from jax.sharding import Mesh, PartitionSpec as P

momentum_decay = 0.9
F32 = jnp.float32
BF16 = jnp.bfloat16

FEAT = ("y", "xh", "core")
TOK = ("xl", "z")
PLANE = FEAT + ("xl",)


def silu_terms(hidden):
    sig = jax.nn.sigmoid(hidden)
    slope = sig * (1.0 + hidden * (1.0 - sig))
    curve = sig * (1.0 - sig) * (2.0 + hidden * (1.0 - 2.0 * sig))
    return (hidden * sig, slope, curve)


def mm(a, b):
    return jnp.dot(a, b, preferred_element_type=F32)


def mm_t(a, b):
    return lax.dot_general(a, b, (((1,), (1,)), ((), ())), preferred_element_type=F32)


def t_mm(a, b):
    return lax.dot_general(a, b, (((0,), (0,)), ((), ())), preferred_element_type=F32)


def swap(x, axis):
    return lax.ppermute(x, axis, [(0, 1), (1, 0)])


def in_order(index, mine, other, axis):
    first = jnp.where(index == 0, mine, other)
    second = jnp.where(index == 0, other, mine)
    return jnp.concatenate([first, second], axis=axis)


def shape(dims, dtype):
    return jax.ShapeDtypeStruct(dims, dtype)


def call(body, name, flops, out_shapes, operands, scratch=()):
    operands = [x if isinstance(x, tuple) else (x, x.shape, None) for x in operands]
    n, m = len(operands), len(out_shapes)
    total = sum(x.size * x.dtype.itemsize for x in [y[0] for y in operands] + list(out_shapes))

    def kernel(*refs):
        sources, targets = refs[:n], refs[n : n + m]
        held, out = refs[n + m : 2 * n + m], refs[2 * n + m : 2 * n + 2 * m]
        in_sems, out_sems = refs[2 * n + 2 * m : 2 * n + 2 * m + 2]
        rest = refs[2 * n + 2 * m + 2 :]
        copies = []
        count = 0
        for i, (unused, unused_dims, pieces) in enumerate(operands):
            copies.append([])
            parts = [(sources[i], None)] if pieces is None else pieces(sources[i])
            for source, at in parts:
                target = held[i] if at is None else held[i].at[at]
                copies[i].append(pltpu.make_async_copy(source, target, in_sems.at[count]))
                copies[i][-1].start()
                count += 1
        here = set()
        sent = []

        def take(i, piece=None):
            for p in range(len(copies[i])) if piece is None else [piece]:
                if (i, p) not in here:
                    copies[i][p].wait()
                    here.add((i, p))
            return held[i]

        def give(i, at=None, source_at=None):
            source = out[i] if at is None else out[i].at[at if source_at is None else source_at]
            target = targets[i] if at is None else targets[i].at[at]
            sent.append(pltpu.make_async_copy(source, target, out_sems.at[len(sent)]))
            sent[-1].start()

        body(take, out, give, *rest)
        for i in range(n):
            take(i)
        for copy in sent:
            copy.wait()

    return pl.pallas_call(
        kernel,
        name=name,
        out_shape=list(out_shapes),
        in_specs=[pl.BlockSpec(memory_space=pltpu.HBM)] * n,
        out_specs=[pl.BlockSpec(memory_space=pltpu.HBM)] * m,
        scratch_shapes=[pltpu.VMEM(dims, x.dtype) for x, dims, unused in operands]
        + [pltpu.VMEM(x.shape, x.dtype) for x in out_shapes]
        + [pltpu.SemaphoreType.DMA((64,)), pltpu.SemaphoreType.DMA((64,))]
        + list(scratch),
        compiler_params=pltpu.CompilerParams(vmem_limit_bytes=64 << 20),
        cost_estimate=pl.CostEstimate(flops=flops, bytes_accessed=total, transcendentals=0),
    )(*[x for x, unused, unused_pieces in operands])


def weight(array, u, n_z):
    rows, half = array.shape[3], array.shape[4] // 2

    def pieces(ref):
        cols = pl.ds(pl.multiple_of(lax.axis_index("xl") * half, half), half)
        return [(ref.at[u, x, :, :, cols], (slice(None), x)) for x in range(2)]

    return array, (n_z, 2, rows, half), pieces


def flat(ref):
    n_z, two, rows, half = ref.shape
    return ref[...].reshape(n_z * two * rows, half)


def flat_block(ref, z):
    return ref[z].reshape(-1, ref.shape[3])


def layer(panels, which):
    n_z, both, block = panels.shape
    half = both // 2
    at = pl.ds(which * half, half)
    part = n_z // 2
    return panels, (n_z, half, block), lambda ref: [
        (ref.at[pl.ds(i * part, part), at], pl.ds(i * part, part)) for i in range(2)
    ]


def slot_of(got, slot):
    n, unused, tokens, share = got.shape
    part = n // 4
    return got, (n, tokens, share), lambda ref: [
        (ref.at[pl.ds(i * part, part), slot], pl.ds(i * part, part)) for i in range(4)
    ]


def gathered(got):
    return [slot_of(x, 0) for x in (got if isinstance(got, tuple) else [got])]


def lay_in_all(take, count, rows):
    if count == 1:
        lay_in(take, 0, rows)
        return
    core = lax.axis_index("core")
    lay_in(take, 0, rows, core)
    lay_in(take, 1, rows, 1 - core)


def row_of(array, u):
    return array, array.shape[1:], lambda ref: [(ref.at[u], None)]


def lay_out(part, chunks, slot, z):
    n_z = chunks.shape[0] // 4
    tokens, share = part.shape[0] // 2, part.shape[1] // 2
    for x in range(2):
        for t in range(2):
            chunks[(x * n_z + z) * 2 + t, slot] = part[
                t * tokens : (t + 1) * tokens, x * share : (x + 1) * share
            ]


def sent_rows(z, n_z):
    return [pl.ds((x * n_z + z - 1) * 2, 4) for x in range(2)] if z % 2 else []


def lay_in(take, i, rows, core=None):
    got = take(i, 0)
    if core is not None:
        n_z = got.shape[0] // 2
        tokens, share = got.shape[1:]
        for chunk in range(got.shape[0]):
            take(i, 4 * chunk // got.shape[0])
            chip, t = chunk // 2, chunk % 2
            z_pair, x = chip % (n_z // 2), chip // (n_z // 2)
            at = pl.multiple_of((4 * z_pair + 2 * core + x) * share, share)
            rows[t * tokens : (t + 1) * tokens, pl.ds(at, share)] = got[chunk]
        return
    n_z = got.shape[0] // 4
    tokens, share = got.shape[1:]
    for x in range(2):
        for z in range(n_z):
            for t in range(2):
                chunk = (x * n_z + z) * 2 + t
                take(i, chunk // n_z)
                at = (2 * z + x) * share
                rows[t * tokens : (t + 1) * tokens, at : at + share] = got[chunk]


def errors(key_rows, w_first, w_second, share):
    updates, tokens, width = key_rows.shape
    full = w_first.shape[2]
    dims = (width // share, updates, tokens, share)
    order = list(reversed(range(updates)))

    def body(take, out, give):
        chunks = out[0]
        for i, u in enumerate(order):
            pre = mm(take(3 * i)[...], take(3 * i + 1)[...])
            act = (pre * jax.nn.sigmoid(pre)).astype(BF16)
            predicted = mm_t(act, take(3 * i + 2)[...]).astype(BF16)
            for f in range(dims[0]):
                chunks[f, u] = predicted[:, f * share : (f + 1) * share]
        for f in range(0, dims[0], 4):
            give(0, pl.ds(f, 4))

    return call(
        body,
        "errors",
        4 * key_rows.size * full,
        [shape(dims, BF16)],
        [row_of(x, u) for u in order for x in (key_rows, w_first, w_second)],
    )[0]


def weigh_out(got, values, rates, chips):
    n, updates, tokens, share = got.shape

    def body(take, out, give):
        parts, spread_out = out
        terms, value, rate = take(0), take(1), take(2)
        for u in reversed(range(updates)):
            total = terms[0, u].astype(F32)
            for i in range(1, n):
                total += terms[i, u].astype(F32)
            rounded = (rate[u] * (total - value[u].astype(F32))).astype(BF16)
            parts[u] = rounded
            if u == updates - 1:
                for i in range(8):
                    spread_out[i, 0] = rounded
                for i in range(0, chips, 8):
                    give(1, pl.ds(i, 8), pl.ds(0, 8))
        give(0)

    return call(
        body,
        "weigh_out",
        got.size,
        [shape(values.shape, BF16), shape((chips, 1, tokens, share), BF16)],
        [got, values, rates],
    )


def outgoing(arrays, u, finals=()):
    n = len(arrays)
    tokens, width = arrays[0].shape[1:]
    quarter = width // 4

    def quarters(ref):
        core = lax.axis_index("core")
        parts = []
        for side in range(2):
            at = pl.multiple_of(core * (2 * quarter) + side * quarter, quarter)
            parts.append((ref.at[u, :, pl.ds(at, quarter)], side))
        return parts

    def body(take, out, give):
        xl = lax.axis_index("xl")
        for i in range(len(finals)):
            half = finals[i].shape[1] // 2
            both = take(i)[...].astype(F32).T.astype(BF16)
            for which in range(2):
                part = both[which * half : (which + 1) * half]

                @pl.when(xl == which)
                def keep(i=i, half=half, part=part):
                    out[3][i * half : (i + 1) * half, :] = part

                @pl.when(xl != which)
                def send(i=i, half=half, part=part):
                    out[2][i * half : (i + 1) * half, :] = part

        if finals:
            give(2)
            give(3)
        for i in range(n):
            for side in range(2):
                out[side][i] = take(len(finals) + i, side)[side]
        give(0)
        give(1)

    turned = [shape((sum(x.shape[1] // 2 for x in finals), finals[0].shape[0]), BF16)] if finals else []
    return call(
        body,
        "outgoing",
        n * tokens * width,
        [shape((n, tokens, quarter), BF16)] * 2 + turned * 2,
        list(finals) + [(x, (2, tokens, quarter), quarters) for x in arrays],
    )


def incoming(to_right, to_left):
    n = lax.axis_size("xh") * 2
    return (
        lax.ppermute(to_right, ("xh", "xl"), [(i, (i + 1) % n) for i in range(n)]),
        lax.ppermute(to_left, ("xh", "xl"), [(i, (i - 1) % n) for i in range(n)]),
    )


def whole(arrays, u, pieces, n_z, other):
    from_left, from_right = pieces
    swapped = after(swap(jnp.concatenate([from_left, from_right], axis=2), "core"), other)
    n = len(arrays)
    tokens, width = arrays[0].shape[1:]
    share = width // (2 * n_z)
    quarter, half = from_left.shape[2], swapped.shape[2]

    def body(take, out, give):
        full = out[0]
        core = lax.axis_index("core")
        xl = lax.axis_index("xl")
        mine = pl.ds(pl.multiple_of(xl * tokens, tokens), tokens)
        other = pl.ds(pl.multiple_of((1 - xl) * tokens, tokens), tokens)
        for i in range(n):
            for x in range(2):
                for z in range(n_z):
                    at = (2 * z + x) * share
                    block = x * half + z * share
                    full[i, mine, at : at + share] = take(i)[:, block : block + share]
            for z in range(n_z):
                at = z * share
                if at < quarter:
                    piece = take(n)[i, :, at : at + share]
                else:
                    piece = take(n + 1)[i, :, at - quarter : at - quarter + share]
                place = pl.multiple_of((2 * z + core) * share, share)
                full[i, other, pl.ds(place, share)] = piece
                place = pl.multiple_of((2 * z + 1 - core) * share, share)
                full[i, other, pl.ds(place, share)] = take(n + 2)[i, :, at : at + share]
            give(0, i)

    return call(
        body,
        "assemble",
        n * tokens * width,
        [shape((n, 2 * tokens, width), BF16)],
        [row_of(x, u) for x in arrays] + [from_left, from_right, swapped],
    )[0]


def forward(held, inner, u):
    tokens, width = held.shape[1:]
    half = inner.shape[4] // 2
    n_z = inner.shape[2]

    def body(take, out, give):
        act, slope, curve = silu_terms(mm(take(0)[...], flat(take(1))))
        for i, value in enumerate([act.astype(BF16), act.T.astype(BF16), slope, curve]):
            out[i][...] = value
            give(i)

    hidden = (tokens, half)
    return call(
        body,
        "forward",
        2 * tokens * width * half,
        [shape(hidden, BF16), shape((half, tokens), BF16), shape(hidden, F32), shape(hidden, F32)],
        [row_of(held, 0), weight(inner, u, n_z)],
    )


def read_out(held, inner, outer, u):
    tokens, width = held.shape[1:]
    half = inner.shape[4] // 2
    n_z = inner.shape[2]

    def body(take, out, give):
        read, slope, unused = silu_terms(mm(take(0)[...], flat(take(2))))
        back_read = mm(take(1)[...], flat(take(3))) * slope
        values = [read.T.astype(BF16), back_read.astype(BF16), back_read.T.astype(BF16)]
        for i, value in enumerate(values):
            out[i][...] = value
            give(i)

    turned = shape((half, tokens), BF16)
    return call(
        body,
        "read_out",
        4 * tokens * width * half,
        [turned, shape((tokens, half), BF16), turned],
        [row_of(held, 1), row_of(held, 2), weight(inner, u, n_z), weight(outer, u, n_z)],
    )


def weigh_in(got, outer, slope, u):
    n_z = outer.shape[2]
    tokens, half = slope.shape
    width = 2 * n_z * outer.shape[3]
    sources = gathered(got)
    count = len(sources)

    def body(take, out, give):
        rows, gated, delta = out
        lay_in_all(take, count, rows)
        give(0)
        total = mm(rows[...], flat(take(count)))
        gated[...] = total
        give(1)
        delta[...] = (total * take(count + 1)[...]).astype(BF16)
        give(2)

    return call(
        body,
        "weigh_in",
        2 * tokens * width * half,
        [shape((tokens, width), BF16), shape((tokens, half), F32), shape((tokens, half), BF16)],
        sources + [weight(outer, u, n_z), slope],
    )


def back(panels, held, slope, act, outer, chunk_shape, u):
    n_z, both, block = panels.shape
    half = both // 2
    tokens = slope.shape[0]

    def body(take, out, give):
        back_delta, back_gated, chunks = out
        rows = take(0)
        total = jnp.zeros((tokens, half), F32)
        for z in range(n_z):
            total += mm_t(rows[:, z * block : (z + 1) * block], take(1, 2 * z // n_z)[z])
        back_delta[...] = total
        give(0)
        gated_b = (total * take(2)[...]).astype(BF16)
        back_gated[...] = gated_b
        give(1)
        act_in, outer_in = take(3)[...], take(4)
        for z in range(n_z):
            part = mm(act_in, take(5, 2 * z // n_z)[z]) + mm_t(gated_b, flat_block(outer_in, z))
            lay_out(part.astype(BF16), chunks, 0, z)
            for rows_out in sent_rows(z, n_z):
                give(2, rows_out)

    hidden = (tokens, half)
    return call(
        body,
        "back",
        6 * held.shape[2] * tokens * half,
        [shape(hidden, F32), shape(hidden, BF16), shape(chunk_shape, BF16)],
        [row_of(held, 0), layer(panels, 0), slope, act, weight(outer, u, n_z), layer(panels, 1)],
    )


def sum_error(got, rates, u):
    n, unused, tokens, share = got.shape

    def body(take, out, give):
        part, spread_out = out
        total = jnp.zeros((tokens, share), F32)
        for i in range(n):
            total += take(0, i * 4 // n)[i].astype(F32)
        rounded = (take(1)[...] * total).astype(BF16)
        part[...] = rounded
        give(0)
        for i in range(8):
            spread_out[i, 0] = rounded
        for i in range(0, n // 2, 8):
            give(1, pl.ds(i, 8), pl.ds(0, 8))

    return call(
        body,
        "error",
        n * tokens * share,
        [shape((tokens, share), BF16), shape((n // 2, 1, tokens, share), BF16)],
        [slot_of(got, 0), row_of(rates, u)],
    )


def base_of(
    panels, weighted, slope, curve, back_delta, gated, back_gated, held, read_t, back_read_t
):
    n_z, both, block = panels.shape
    tokens, half = slope.shape

    def body(take, out, give):
        pre, terms = out
        rows = take(0)
        total = jnp.zeros((tokens, half), F32)
        for z in range(n_z):
            total += mm_t(rows[:, z * block : (z + 1) * block], take(1, 2 * z // n_z)[z])
        pre[...] = total * take(2)[...] + take(3)[...] * take(4)[...] * take(5)[...]
        give(0)
        back_gated_t = take(6)[...].astype(F32).T.astype(BF16)
        read_in, back_read_in = take(7)[...], take(8)[...]
        reads, cots = take(9), take(10)
        for z in range(n_z):
            cols = slice(z * block, (z + 1) * block)
            terms[z, :half, :] = mm(back_read_in, reads[:, cols]).astype(BF16)
            second = mm(back_gated_t, rows[:, cols]) + mm(read_in, cots[:, cols])
            terms[z, half:, :] = second.astype(BF16)
            give(1, z)

    return call(
        body,
        "base",
        4 * weighted.size * both,
        [shape(slope.shape, F32), shape(panels.shape, BF16)],
        [weighted, layer(panels, 1), slope, curve, back_delta, gated, back_gated]
        + [read_t, back_read_t, row_of(held, 1), row_of(held, 2)],
    )


def terms_of(got, base_pre, base_terms, slope, outer, held, act_t, u):
    tokens, half = slope.shape
    n_z = outer.shape[2]
    width = held.shape[2]
    block = width // n_z
    sources = gathered(got)
    count = len(sources)

    def body(take_any, out, give, back_out):
        back_pre, terms = out
        lay_in_all(take_any, count, back_out)

        def take(i):
            return take_any(count + i)

        pre = take(2)[...] + mm(back_out[...], flat(take(0))) * take(1)[...]
        back_pre[...] = pre.astype(BF16)
        give(0)
        pre_t = pre.T.astype(BF16)
        act_in, key, base = take(3)[...], take(4), take(5)
        for z in range(n_z):
            cols = slice(z * block, (z + 1) * block)
            first = mm(pre_t, key[:, cols]) + base[z, :half, :].astype(F32)
            terms[z, :half, :] = first.astype(BF16)
            second = mm(act_in, back_out[:, cols]) + base[z, half:, :].astype(F32)
            terms[z, half:, :] = second.astype(BF16)
            give(1, z)

    return call(
        body,
        "terms",
        6 * tokens * width * half,
        [shape((tokens, half), BF16), shape((n_z, 2 * half, block), BF16)],
        sources
        + [weight(outer, u, n_z), slope, base_pre, act_t, row_of(held, 0), base_terms],
        scratch=[pltpu.VMEM((tokens, width), BF16)],
    )


def spread(parts, n_z, share):
    operands = []
    for part in parts:
        if isinstance(part, list):
            for pair in part:
                operands.extend(pair)
        else:
            operands.append(part)
    tokens = share
    dims = (4 * n_z, len(parts), tokens, share)

    def body(take, out, give):
        chunks = out[0]
        for z in range(n_z):
            at = 0
            for slot, part in enumerate(parts):
                if not isinstance(part, list):
                    for x in range(2):
                        for t in range(2):
                            chunks[(x * n_z + z) * 2 + t, slot] = take(at)[...]
                    at += 1
                    continue
                total = None
                for rows, operand in part:
                    if len(operand[1]) == 3:
                        term = mm(take(at)[...], take(at + 1, 2 * z // n_z)[z])
                    else:
                        term = mm_t(take(at)[...], flat_block(take(at + 1), z))
                    total = term if total is None else total + term
                    at += 2
                lay_out(total.astype(BF16), chunks, slot, z)
            for rows_out in sent_rows(z, n_z):
                give(0, rows_out)

    flops = sum(4 * tokens * math.prod(x[1]) for x in operands if isinstance(x, tuple))
    return call(body, "spread", flops, [shape(dims, BF16)], operands)[0]


def exchange(chunks):
    return lax.all_to_all(chunks, PLANE, 0, 0, tiled=True)


def gather(chunks, beside):
    mine = after(lax.all_to_all(chunks, ("y", "xh", "xl"), 0, 0, tiled=True), beside)
    return mine, swap(mine, "core")


def summed(got, slot):
    return jnp.sum(got[:, slot].astype(F32), axis=0)


def after(value, other):
    return lax.optimization_barrier((value, other))[0]


def on_device(
    key_rows,
    value_rows,
    queries,
    output_cot,
    token_rates,
    w_first,
    w_second,
    final_first,
    final_second,
):
    updates, own_tokens, d_width = key_rows.shape
    share = value_rows.shape[2]
    half = w_first.shape[2] // 2
    n_z = lax.axis_size("z")
    block_tokens = 2 * own_tokens * n_z
    xl = lax.axis_index("xl")
    last = updates - 1
    plane = lax.axis_size(PLANE)

    def part_of(total, which):
        return lax.dynamic_index_in_dim(total.reshape(2 * half, 2, -1), which, 1, keepdims=False)

    rates = jnp.broadcast_to((token_rates / block_tokens)[:, :, None], value_rows.shape)
    inner = w_first.reshape(updates, 2, n_z, -1, 2 * half)
    outer = w_second.reshape(updates, 2, n_z, -1, 2 * half)

    rows = [key_rows, queries, output_cot]

    to_right, to_left, other_final, own_final = outgoing(rows, last, [final_first, final_second])
    other_final = swap(other_final, "xl")
    pieces = incoming(to_right, to_left)
    error_chunks = errors(key_rows, w_first, w_second, share)
    other_final = after(other_final, (error_chunks, pieces))
    start = in_order(xl, own_final, other_final, 1)
    panels = lax.all_gather(-start, "z", axis=0, tiled=False)

    got = lax.all_to_all(after(error_chunks, (start, rates)), FEAT, 0, 0, tiled=True)
    weighted_part, chunks = weigh_out(got, value_rows, rates, plane // 2)
    held = [None] * updates
    hidden = [None] * updates
    read_list = [None] * updates
    held[last] = whole(rows, last, pieces, n_z, weighted_part)
    hidden[last] = forward(held[last], inner, last)
    got = gather(chunks, hidden[last])
    read_list[last] = read_out(after(held[last], panels), inner, outer, last)

    next_in = weigh_in(got, outer, hidden[last][2], last)
    carry = start.astype(F32)
    moment = carry
    totals = []
    key_list = [None] * updates
    value_list = [None] * updates
    query_list = [None] * updates
    for u in reversed(range(updates)):
        act, act_t, slope, curve = hidden[u]
        weighted, gated, delta = next_in
        back_delta, back_gated, chunks = back(
            panels, held[u], slope, act, outer, (plane, 1, own_tokens, share), u
        )
        read_t, back_read, back_read_t = read_list[u]
        base_pre, base_terms = base_of(
            panels,
            weighted,
            slope,
            curve,
            back_delta,
            gated,
            back_gated,
            held[u],
            read_t,
            back_read_t,
        )
        got = after(exchange(after(chunks, got)), (gated, read_list[u]))
        back_part, chunks = sum_error(got, rates, u)
        value_list[u] = -back_part
        beside = [base_pre, base_terms]
        if u > 0:
            chunks_now = spread(
                [
                    (weighted_part, (own_tokens, share), lambda ref: [(ref.at[u - 1], None)]),
                    [(back_read, weight(inner, u, n_z))],
                ],
                n_z,
                share,
            )
            beside.append(chunks_now)
        got = gather(chunks, beside)
        back_pre, terms = terms_of(
            got, base_pre, base_terms, slope, outer, held[u], act_t, u
        )
        key_parts = [(delta, layer(panels, 0)), (back_pre, weight(inner, u, n_z))]
        total = lax.psum_scatter(terms, "z", scatter_dimension=0, tiled=True)[0]
        if u > 0:
            got = exchange(after(chunks_now, terms))
            chunks = spread([key_parts], n_z, share)
            sent = outgoing([after(x, terms) for x in rows], u - 1)
            total, got, chunks, sent = lax.optimization_barrier((total, got, chunks, sent))
            totals.append(total)
            carry = carry + total.astype(F32)
            moment = carry + momentum_decay * moment
            panel = (-moment).astype(BF16)
            panels = lax.all_gather(panel, "z", axis=0, tiled=False)
            pieces = incoming(*[after(x, panel) for x in sent])
            held[u - 1] = whole(rows, u - 1, pieces, n_z, panel)
            sums = exchange(after(chunks, held[u - 1]))
            query_list[u] = summed(after(got, panel), 1).astype(BF16)
            hidden[u - 1] = forward(held[u - 1], inner, u - 1)
            read_list[u - 1] = read_out(held[u - 1], inner, outer, u - 1)
            next_in = weigh_in(after(got, panel), outer, hidden[u - 1][2], u - 1)
            panels, sums, next_in = lax.optimization_barrier((panels, sums, next_in))
            key_list[u] = summed(sums, 0).astype(BF16)
        else:
            parts = [key_parts, [(back_read, weight(inner, u, n_z))]]
            chunks = spread(parts, n_z, share)
            sent = [swap(after(part_of(x, 1 - xl), terms), "xl") for x in totals]
            sums = exchange(after(chunks, sent))
            totals.append(total)
            sent.append(swap(part_of(total, 1 - xl), "xl"))
            key_list[u] = summed(sums, 0).astype(BF16)
            query_list[u] = summed(sums, 1).astype(BF16)

    grad_first = final_first.astype(F32)
    grad_second = final_second.astype(F32)
    for total, other in zip(totals, sent):
        kept, other = part_of(total, xl).T, other.T
        grad_first = grad_first + in_order(xl, kept[:, :half], other[:, :half], 1)
        grad_second = grad_second + in_order(xl, kept[:, half:], other[:, half:], 1)
    return (
        jnp.stack(key_list),
        jnp.stack(value_list),
        jnp.stack(query_list),
        grad_first,
        grad_second,
    )


def solution(mesh):
    n_feat, n_tok = mesh.devices.shape
    fine = Mesh(
        mesh.devices.reshape(n_feat // 4, 2, 2, 2, n_tok // 2), ("y", "xh", "core", "xl", "z")
    )
    return jax.shard_map(
        on_device,
        mesh=fine,
        in_specs=(
            P(None, TOK, None),
            P(None, TOK, FEAT),
            P(None, TOK, None),
            P(None, TOK, None),
            P(None, TOK),
            P(None, None, FEAT),
            P(None, None, FEAT),
            P(TOK, FEAT),
            P(TOK, FEAT),
        ),
        out_specs=(
            P(None, TOK, FEAT),
            P(None, TOK, FEAT),
            P(None, TOK, FEAT),
            P(TOK, FEAT),
            P(TOK, FEAT),
        ),
        check_vma=False,
    )
```

```python
import math

import jax
import jax.numpy as jnp
from jax import lax
from jax.experimental import pallas as pl
from jax.experimental.pallas import tpu as pltpu
from jax.sharding import Mesh, PartitionSpec as P

momentum_decay = 0.9
F32 = jnp.float32
BF16 = jnp.bfloat16

FEAT = ("y", "xh", "core")
TOK = ("xl", "z")
PLANE = FEAT + ("xl",)


def silu_terms(hidden):
    sig = jax.nn.sigmoid(hidden)
    slope = sig * (1.0 + hidden * (1.0 - sig))
    curve = sig * (1.0 - sig) * (2.0 + hidden * (1.0 - 2.0 * sig))
    return (hidden * sig, slope, curve)


def mm(a, b):
    return jnp.dot(a, b, preferred_element_type=F32)


def mm_t(a, b):
    return lax.dot_general(a, b, (((1,), (1,)), ((), ())), preferred_element_type=F32)


def t_mm(a, b):
    return lax.dot_general(a, b, (((0,), (0,)), ((), ())), preferred_element_type=F32)


def swap(x, axis):
    return lax.ppermute(x, axis, [(0, 1), (1, 0)])


def in_order(index, mine, other, axis):
    first = jnp.where(index == 0, mine, other)
    second = jnp.where(index == 0, other, mine)
    return jnp.concatenate([first, second], axis=axis)


def shape(dims, dtype):
    return jax.ShapeDtypeStruct(dims, dtype)


def call(body, name, flops, out_shapes, operands, scratch=()):
    operands = [x if isinstance(x, tuple) else (x, x.shape, None) for x in operands]
    n, m = len(operands), len(out_shapes)
    total = sum(x.size * x.dtype.itemsize for x in [y[0] for y in operands] + list(out_shapes))

    def kernel(*refs):
        sources, targets = refs[:n], refs[n : n + m]
        held, out = refs[n + m : 2 * n + m], refs[2 * n + m : 2 * n + 2 * m]
        in_sems, out_sems = refs[2 * n + 2 * m : 2 * n + 2 * m + 2]
        rest = refs[2 * n + 2 * m + 2 :]
        copies = []
        count = 0
        for i, (unused, unused_dims, pieces) in enumerate(operands):
            copies.append([])
            parts = [(sources[i], None)] if pieces is None else pieces(sources[i])
            for source, at in parts:
                target = held[i] if at is None else held[i].at[at]
                copies[i].append(pltpu.make_async_copy(source, target, in_sems.at[count]))
                copies[i][-1].start()
                count += 1
        here = set()
        sent = []

        def take(i, piece=None):
            for p in range(len(copies[i])) if piece is None else [piece]:
                if (i, p) not in here:
                    copies[i][p].wait()
                    here.add((i, p))
            return held[i]

        def give(i, at=None, source_at=None):
            source = out[i] if at is None else out[i].at[at if source_at is None else source_at]
            target = targets[i] if at is None else targets[i].at[at]
            sent.append(pltpu.make_async_copy(source, target, out_sems.at[len(sent)]))
            sent[-1].start()

        body(take, out, give, *rest)
        for i in range(n):
            take(i)
        for copy in sent:
            copy.wait()

    return pl.pallas_call(
        kernel,
        name=name,
        out_shape=list(out_shapes),
        in_specs=[pl.BlockSpec(memory_space=pltpu.HBM)] * n,
        out_specs=[pl.BlockSpec(memory_space=pltpu.HBM)] * m,
        scratch_shapes=[pltpu.VMEM(dims, x.dtype) for x, dims, unused in operands]
        + [pltpu.VMEM(x.shape, x.dtype) for x in out_shapes]
        + [pltpu.SemaphoreType.DMA((64,)), pltpu.SemaphoreType.DMA((64,))]
        + list(scratch),
        compiler_params=pltpu.CompilerParams(vmem_limit_bytes=64 << 20),
        cost_estimate=pl.CostEstimate(flops=flops, bytes_accessed=total, transcendentals=0),
    )(*[x for x, unused, unused_pieces in operands])


def weight(array, u, n_z):
    rows, half = array.shape[3], array.shape[4] // 2

    def pieces(ref):
        cols = pl.ds(pl.multiple_of(lax.axis_index("xl") * half, half), half)
        return [(ref.at[u, x, :, :, cols], (slice(None), x)) for x in range(2)]

    return array, (n_z, 2, rows, half), pieces


def flat(ref):
    n_z, two, rows, half = ref.shape
    return ref[...].reshape(n_z * two * rows, half)


def flat_block(ref, z):
    return ref[z].reshape(-1, ref.shape[3])


def layer(panels, which):
    n_z, both, block = panels.shape
    half = both // 2
    at = pl.ds(which * half, half)
    part = n_z // 2
    return panels, (n_z, half, block), lambda ref: [
        (ref.at[pl.ds(i * part, part), at], pl.ds(i * part, part)) for i in range(2)
    ]


def slot_of(got, slot):
    n, unused, tokens, share = got.shape
    part = n // 4
    return got, (n, tokens, share), lambda ref: [
        (ref.at[pl.ds(i * part, part), slot], pl.ds(i * part, part)) for i in range(4)
    ]


def gathered(got):
    return [slot_of(x, 0) for x in (got if isinstance(got, tuple) else [got])]


def lay_in_all(take, count, rows):
    if count == 1:
        lay_in(take, 0, rows)
        return
    core = lax.axis_index("core")
    lay_in(take, 0, rows, core)
    lay_in(take, 1, rows, 1 - core)


def scaled(rates, u, tokens, share, n_z):
    row = rates[u : u + 1, :] / (2 * tokens * n_z)
    return jnp.broadcast_to(row, (share, tokens)).T


def row_of(array, u):
    return array, array.shape[1:], lambda ref: [(ref.at[u], None)]


def lay_out(part, chunks, slot, z):
    n_z = chunks.shape[0] // 4
    tokens, share = part.shape[0] // 2, part.shape[1] // 2
    for x in range(2):
        for t in range(2):
            chunks[(x * n_z + z) * 2 + t, slot] = part[
                t * tokens : (t + 1) * tokens, x * share : (x + 1) * share
            ]


def sent_rows(z, n_z):
    return [pl.ds((x * n_z + z - 1) * 2, 4) for x in range(2)] if z % 2 else []


def lay_in(take, i, rows, core=None):
    got = take(i, 0)
    if core is not None:
        n_z = got.shape[0] // 2
        tokens, share = got.shape[1:]
        for chunk in range(got.shape[0]):
            take(i, 4 * chunk // got.shape[0])
            chip, t = chunk // 2, chunk % 2
            z_pair, x = chip % (n_z // 2), chip // (n_z // 2)
            at = pl.multiple_of((4 * z_pair + 2 * core + x) * share, share)
            rows[t * tokens : (t + 1) * tokens, pl.ds(at, share)] = got[chunk]
        return
    n_z = got.shape[0] // 4
    tokens, share = got.shape[1:]
    for x in range(2):
        for z in range(n_z):
            for t in range(2):
                chunk = (x * n_z + z) * 2 + t
                take(i, chunk // n_z)
                at = (2 * z + x) * share
                rows[t * tokens : (t + 1) * tokens, at : at + share] = got[chunk]


def errors(key_rows, w_first, w_second, share):
    updates, tokens, width = key_rows.shape
    full = w_first.shape[2]
    dims = (width // share, updates, tokens, share)
    order = list(reversed(range(updates)))

    def body(take, out, give):
        chunks = out[0]
        for i, u in enumerate(order):
            pre = mm(take(3 * i)[...], take(3 * i + 1)[...])
            act = (pre * jax.nn.sigmoid(pre)).astype(BF16)
            predicted = mm_t(act, take(3 * i + 2)[...]).astype(BF16)
            for f in range(dims[0]):
                chunks[f, u] = predicted[:, f * share : (f + 1) * share]
        for f in range(0, dims[0], 4):
            give(0, pl.ds(f, 4))

    return call(
        body,
        "errors",
        4 * key_rows.size * full,
        [shape(dims, BF16)],
        [row_of(x, u) for u in order for x in (key_rows, w_first, w_second)],
    )[0]


def weigh_out(got, values, rates, chips, n_z):
    n, updates, tokens, share = got.shape

    def body(take, out, give):
        parts, spread_out = out
        terms, value, rate = take(0), take(1), take(2)
        for u in reversed(range(updates)):
            total = terms[0, u].astype(F32)
            for i in range(1, n):
                total += terms[i, u].astype(F32)
            error = total - value[u].astype(F32)
            rounded = (scaled(rate, u, tokens, share, n_z) * error).astype(BF16)
            parts[u] = rounded
            if u == updates - 1:
                for i in range(8):
                    spread_out[i, 0] = rounded
                for i in range(0, chips, 8):
                    give(1, pl.ds(i, 8), pl.ds(0, 8))
        give(0)

    return call(
        body,
        "weigh_out",
        got.size,
        [shape(values.shape, BF16), shape((chips, 1, tokens, share), BF16)],
        [got, values, rates],
    )


def outgoing(arrays, u, finals=()):
    n = len(arrays)
    tokens, width = arrays[0].shape[1:]
    quarter = width // 4

    def quarters(ref):
        core = lax.axis_index("core")
        parts = []
        for side in range(2):
            at = pl.multiple_of(core * (2 * quarter) + side * quarter, quarter)
            parts.append((ref.at[u, :, pl.ds(at, quarter)], side))
        return parts

    def body(take, out, give):
        xl = lax.axis_index("xl")
        for i in range(len(finals)):
            half = finals[i].shape[1] // 2
            both = take(i)[...].astype(F32).T.astype(BF16)
            for which in range(2):
                part = both[which * half : (which + 1) * half]

                @pl.when(xl == which)
                def keep(i=i, half=half, part=part):
                    out[3][i * half : (i + 1) * half, :] = part

                @pl.when(xl != which)
                def send(i=i, half=half, part=part):
                    out[2][i * half : (i + 1) * half, :] = part

        if finals:
            give(2)
            give(3)
        for i in range(n):
            for side in range(2):
                out[side][i] = take(len(finals) + i, side)[side]
        give(0)
        give(1)

    turned = [shape((sum(x.shape[1] // 2 for x in finals), finals[0].shape[0]), BF16)] if finals else []
    return call(
        body,
        "outgoing",
        n * tokens * width,
        [shape((n, tokens, quarter), BF16)] * 2 + turned * 2,
        list(finals) + [(x, (2, tokens, quarter), quarters) for x in arrays],
    )


def incoming(to_right, to_left):
    n = lax.axis_size("xh") * 2
    return (
        lax.ppermute(to_right, ("xh", "xl"), [(i, (i + 1) % n) for i in range(n)]),
        lax.ppermute(to_left, ("xh", "xl"), [(i, (i - 1) % n) for i in range(n)]),
    )


def from_core(pieces):
    return swap(jnp.concatenate(pieces, axis=2), "core")


def whole(arrays, u, pieces, swapped, n_z):
    from_left, from_right = pieces
    n = len(arrays)
    tokens, width = arrays[0].shape[1:]
    share = width // (2 * n_z)
    quarter, half = from_left.shape[2], swapped.shape[2]

    def body(take, out, give):
        full = out[0]
        core = lax.axis_index("core")
        xl = lax.axis_index("xl")
        mine = pl.ds(pl.multiple_of(xl * tokens, tokens), tokens)
        other = pl.ds(pl.multiple_of((1 - xl) * tokens, tokens), tokens)
        for i in range(n):
            for x in range(2):
                for z in range(n_z):
                    at = (2 * z + x) * share
                    block = x * half + z * share
                    full[i, mine, at : at + share] = take(i)[:, block : block + share]
            for z in range(n_z):
                at = z * share
                if at < quarter:
                    piece = take(n)[i, :, at : at + share]
                else:
                    piece = take(n + 1)[i, :, at - quarter : at - quarter + share]
                place = pl.multiple_of((2 * z + core) * share, share)
                full[i, other, pl.ds(place, share)] = piece
                place = pl.multiple_of((2 * z + 1 - core) * share, share)
                full[i, other, pl.ds(place, share)] = take(n + 2)[i, :, at : at + share]
            give(0, i)

    return call(
        body,
        "assemble",
        n * tokens * width,
        [shape((n, 2 * tokens, width), BF16)],
        [row_of(x, u) for x in arrays] + [from_left, from_right, swapped],
    )[0]


def forward(held, inner, u):
    tokens, width = held.shape[1:]
    half = inner.shape[4] // 2
    n_z = inner.shape[2]

    def body(take, out, give):
        act, slope, curve = silu_terms(mm(take(0)[...], flat(take(1))))
        for i, value in enumerate([act.astype(BF16), act.T.astype(BF16), slope, curve]):
            out[i][...] = value
            give(i)

    hidden = (tokens, half)
    return call(
        body,
        "forward",
        2 * tokens * width * half,
        [shape(hidden, BF16), shape((half, tokens), BF16), shape(hidden, F32), shape(hidden, F32)],
        [row_of(held, 0), weight(inner, u, n_z)],
    )


def read_out(held, inner, outer, u):
    tokens, width = held.shape[1:]
    half = inner.shape[4] // 2
    n_z = inner.shape[2]

    def body(take, out, give):
        read, slope, unused = silu_terms(mm(take(0)[...], flat(take(2))))
        back_read = mm(take(1)[...], flat(take(3))) * slope
        values = [read.T.astype(BF16), back_read.astype(BF16), back_read.T.astype(BF16)]
        for i, value in enumerate(values):
            out[i][...] = value
            give(i)

    turned = shape((half, tokens), BF16)
    return call(
        body,
        "read_out",
        4 * tokens * width * half,
        [turned, shape((tokens, half), BF16), turned],
        [row_of(held, 1), row_of(held, 2), weight(inner, u, n_z), weight(outer, u, n_z)],
    )


def weigh_in(got, outer, slope, u):
    n_z = outer.shape[2]
    tokens, half = slope.shape
    width = 2 * n_z * outer.shape[3]
    sources = gathered(got)
    count = len(sources)

    def body(take, out, give):
        rows, gated, delta = out
        lay_in_all(take, count, rows)
        give(0)
        total = mm(rows[...], flat(take(count)))
        gated[...] = total
        give(1)
        delta[...] = (total * take(count + 1)[...]).astype(BF16)
        give(2)

    return call(
        body,
        "weigh_in",
        2 * tokens * width * half,
        [shape((tokens, width), BF16), shape((tokens, half), F32), shape((tokens, half), BF16)],
        sources + [weight(outer, u, n_z), slope],
    )


def back(panels, held, slope, act, outer, chunk_shape, u):
    n_z, both, block = panels.shape
    half = both // 2
    tokens = slope.shape[0]

    def body(take, out, give):
        back_delta, back_gated, chunks = out
        rows = take(0)
        total = jnp.zeros((tokens, half), F32)
        for z in range(n_z):
            total += mm_t(rows[:, z * block : (z + 1) * block], take(1, 2 * z // n_z)[z])
        back_delta[...] = total
        give(0)
        gated_b = (total * take(2)[...]).astype(BF16)
        back_gated[...] = gated_b
        give(1)
        act_in, outer_in = take(3)[...], take(4)
        for z in range(n_z):
            part = mm(act_in, take(5, 2 * z // n_z)[z]) + mm_t(gated_b, flat_block(outer_in, z))
            lay_out(part.astype(BF16), chunks, 0, z)
            for rows_out in sent_rows(z, n_z):
                give(2, rows_out)

    hidden = (tokens, half)
    return call(
        body,
        "back",
        6 * held.shape[2] * tokens * half,
        [shape(hidden, F32), shape(hidden, BF16), shape(chunk_shape, BF16)],
        [row_of(held, 0), layer(panels, 0), slope, act, weight(outer, u, n_z), layer(panels, 1)],
    )


def sum_error(got, rates, u, n_z):
    n, unused, tokens, share = got.shape

    def body(take, out, give):
        part, spread_out = out
        total = jnp.zeros((tokens, share), F32)
        for i in range(n):
            total += take(0, i * 4 // n)[i].astype(F32)
        rounded = (scaled(take(1), u, tokens, share, n_z) * total).astype(BF16)
        part[...] = rounded
        give(0)
        for i in range(8):
            spread_out[i, 0] = rounded
        for i in range(0, n // 2, 8):
            give(1, pl.ds(i, 8), pl.ds(0, 8))

    return call(
        body,
        "error",
        n * tokens * share,
        [shape((tokens, share), BF16), shape((n // 2, 1, tokens, share), BF16)],
        [slot_of(got, 0), rates],
    )


def base_of(
    panels, weighted, slope, curve, back_delta, gated, back_gated, held, read_t, back_read_t
):
    n_z, both, block = panels.shape
    tokens, half = slope.shape

    def body(take, out, give):
        pre, terms = out
        rows = take(0)
        total = jnp.zeros((tokens, half), F32)
        for z in range(n_z):
            total += mm_t(rows[:, z * block : (z + 1) * block], take(1, 2 * z // n_z)[z])
        pre[...] = total * take(2)[...] + take(3)[...] * take(4)[...] * take(5)[...]
        give(0)
        back_gated_t = take(6)[...].astype(F32).T.astype(BF16)
        read_in, back_read_in = take(7)[...], take(8)[...]
        reads, cots = take(9), take(10)
        for z in range(n_z):
            cols = slice(z * block, (z + 1) * block)
            terms[z, :half, :] = mm(back_read_in, reads[:, cols]).astype(BF16)
            second = mm(back_gated_t, rows[:, cols]) + mm(read_in, cots[:, cols])
            terms[z, half:, :] = second.astype(BF16)
            give(1, z)

    return call(
        body,
        "base",
        4 * weighted.size * both,
        [shape(slope.shape, F32), shape(panels.shape, BF16)],
        [weighted, layer(panels, 1), slope, curve, back_delta, gated, back_gated]
        + [read_t, back_read_t, row_of(held, 1), row_of(held, 2)],
    )


def terms_of(got, base_pre, base_terms, slope, outer, held, act_t, u):
    tokens, half = slope.shape
    n_z = outer.shape[2]
    width = held.shape[2]
    block = width // n_z
    sources = gathered(got)
    count = len(sources)

    def body(take_any, out, give, back_out):
        back_pre, terms = out
        lay_in_all(take_any, count, back_out)

        def take(i):
            return take_any(count + i)

        pre = take(2)[...] + mm(back_out[...], flat(take(0))) * take(1)[...]
        back_pre[...] = pre.astype(BF16)
        give(0)
        pre_t = pre.T.astype(BF16)
        act_in, key, base = take(3)[...], take(4), take(5)
        for z in range(n_z):
            cols = slice(z * block, (z + 1) * block)
            first = mm(pre_t, key[:, cols]) + base[z, :half, :].astype(F32)
            terms[z, :half, :] = first.astype(BF16)
            second = mm(act_in, back_out[:, cols]) + base[z, half:, :].astype(F32)
            terms[z, half:, :] = second.astype(BF16)
            give(1, z)

    return call(
        body,
        "terms",
        6 * tokens * width * half,
        [shape((tokens, half), BF16), shape((n_z, 2 * half, block), BF16)],
        sources
        + [weight(outer, u, n_z), slope, base_pre, act_t, row_of(held, 0), base_terms],
        scratch=[pltpu.VMEM((tokens, width), BF16)],
    )


def spread(parts, n_z, share):
    operands = []
    for part in parts:
        if isinstance(part, list):
            for pair in part:
                operands.extend(pair)
        else:
            operands.append(part)
    tokens = share
    dims = (4 * n_z, len(parts), tokens, share)

    def body(take, out, give):
        chunks = out[0]
        for z in range(n_z):
            at = 0
            for slot, part in enumerate(parts):
                if not isinstance(part, list):
                    for x in range(2):
                        for t in range(2):
                            chunks[(x * n_z + z) * 2 + t, slot] = take(at)[...]
                    at += 1
                    continue
                total = None
                for rows, operand in part:
                    if len(operand[1]) == 3:
                        term = mm(take(at)[...], take(at + 1, 2 * z // n_z)[z])
                    else:
                        term = mm_t(take(at)[...], flat_block(take(at + 1), z))
                    total = term if total is None else total + term
                    at += 2
                lay_out(total.astype(BF16), chunks, slot, z)
            for rows_out in sent_rows(z, n_z):
                give(0, rows_out)

    flops = sum(4 * tokens * math.prod(x[1]) for x in operands if isinstance(x, tuple))
    return call(body, "spread", flops, [shape(dims, BF16)], operands)[0]


def exchange(chunks):
    return lax.all_to_all(chunks, PLANE, 0, 0, tiled=True)


def gather(chunks, beside):
    mine = after(lax.all_to_all(chunks, ("y", "xh", "xl"), 0, 0, tiled=True), beside)
    return mine, swap(mine, "core")


def summed(got, slot):
    return jnp.sum(got[:, slot].astype(F32), axis=0)


def after(value, other):
    return lax.optimization_barrier((value, other))[0]


def on_device(
    key_rows,
    value_rows,
    queries,
    output_cot,
    token_rates,
    w_first,
    w_second,
    final_first,
    final_second,
):
    updates, own_tokens, d_width = key_rows.shape
    share = value_rows.shape[2]
    half = w_first.shape[2] // 2
    n_z = lax.axis_size("z")
    xl = lax.axis_index("xl")
    last = updates - 1
    plane = lax.axis_size(PLANE)

    def part_of(total, which):
        return lax.dynamic_index_in_dim(total.reshape(2 * half, 2, -1), which, 1, keepdims=False)

    inner = w_first.reshape(updates, 2, n_z, -1, 2 * half)
    outer = w_second.reshape(updates, 2, n_z, -1, 2 * half)

    rows = [key_rows, queries, output_cot]

    to_right, to_left, other_final, own_final = outgoing(rows, last, [final_first, final_second])
    pieces = incoming(to_right, to_left)
    other_final = swap(other_final, "xl")
    error_chunks = errors(key_rows, w_first, w_second, share)
    other_final = after(other_final, (error_chunks, pieces))
    start = in_order(xl, own_final, other_final, 1)
    panels = lax.all_gather(-start, "z", axis=0, tiled=False)

    got = lax.all_to_all(after(error_chunks, start), FEAT, 0, 0, tiled=True)
    weighted_part, chunks = weigh_out(got, value_rows, token_rates, plane // 2, n_z)
    held = [None] * updates
    hidden = [None] * updates
    read_list = [None] * updates
    swapped = after(from_core(pieces), weighted_part)
    held[last] = whole(rows, last, pieces, swapped, n_z)
    hidden[last] = forward(held[last], inner, last)
    got = gather(chunks, hidden[last])
    read_list[last] = read_out(after(held[last], panels), inner, outer, last)

    next_in = weigh_in(got, outer, hidden[last][2], last)
    carry = start.astype(F32)
    moment = carry
    totals = []
    parts_sent = []
    key_list = [None] * updates
    value_list = [None] * updates
    query_list = [None] * updates
    for u in reversed(range(updates)):
        act, act_t, slope, curve = hidden[u]
        weighted, gated, delta = next_in
        back_delta, back_gated, chunks = back(
            panels, held[u], slope, act, outer, (plane, 1, own_tokens, share), u
        )
        read_t, back_read, back_read_t = read_list[u]
        base_pre, base_terms = base_of(
            panels,
            weighted,
            slope,
            curve,
            back_delta,
            gated,
            back_gated,
            held[u],
            read_t,
            back_read_t,
        )
        got = after(exchange(after(chunks, got)), (gated, read_list[u]))
        back_part, chunks = sum_error(got, token_rates, u, n_z)
        value_list[u] = -back_part
        beside = [base_pre, base_terms]
        if u > 0:
            chunks_now = spread(
                [
                    (weighted_part, (own_tokens, share), lambda ref: [(ref.at[u - 1], None)]),
                    [(back_read, weight(inner, u, n_z))],
                ],
                n_z,
                share,
            )
            beside.append(chunks_now)
        got = gather(chunks, beside)
        back_pre, terms = terms_of(
            got, base_pre, base_terms, slope, outer, held[u], act_t, u
        )
        key_parts = [(delta, layer(panels, 0)), (back_pre, weight(inner, u, n_z))]
        total = lax.psum_scatter(terms, "z", scatter_dimension=0, tiled=True)[0]
        if u > 0:
            got = exchange(after(chunks_now, terms))
            chunks = spread([key_parts], n_z, share)
            sent = outgoing([after(x, terms) for x in rows], u - 1)
            total, got, chunks, sent = lax.optimization_barrier((total, got, chunks, sent))
            totals.append(total)
            carry = carry + total.astype(F32)
            moment = carry + momentum_decay * moment
            panel = (-moment).astype(BF16)
            panels = lax.all_gather(panel, "z", axis=0, tiled=False)
            pieces = incoming(*[after(x, panel) for x in sent])
            swapped = from_core(pieces)
            sums = exchange(after(chunks, swapped))
            held[u - 1] = whole(rows, u - 1, pieces, swapped, n_z)
            query_list[u] = summed(after(got, panel), 1).astype(BF16)
            hidden[u - 1] = forward(held[u - 1], inner, u - 1)
            read_list[u - 1] = read_out(held[u - 1], inner, outer, u - 1)
            next_in = weigh_in(after(got, panel), outer, hidden[u - 1][2], u - 1)
            leaving = part_of(total, 1 - xl)
            panels, sums, next_in, leaving = lax.optimization_barrier(
                (panels, sums, next_in, leaving)
            )
            parts_sent.append(leaving)
            key_list[u] = summed(sums, 0).astype(BF16)
        else:
            parts = [key_parts, [(back_read, weight(inner, u, n_z))]]
            chunks = spread(parts, n_z, share)
            sent = [swap(after(x, terms), "xl") for x in parts_sent]
            sums = exchange(after(chunks, sent))
            totals.append(total)
            sent.append(swap(part_of(total, 1 - xl), "xl"))
            key_list[u] = summed(sums, 0).astype(BF16)
            query_list[u] = summed(sums, 1).astype(BF16)

    grad_first = final_first.astype(F32)
    grad_second = final_second.astype(F32)
    for total, other in zip(totals, sent):
        kept, other = part_of(total, xl).T, other.T
        grad_first = grad_first + in_order(xl, kept[:, :half], other[:, :half], 1)
        grad_second = grad_second + in_order(xl, kept[:, half:], other[:, half:], 1)
    return (
        jnp.stack(key_list),
        jnp.stack(value_list),
        jnp.stack(query_list),
        grad_first,
        grad_second,
    )


def solution(mesh):
    n_feat, n_tok = mesh.devices.shape
    fine = Mesh(
        mesh.devices.reshape(n_feat // 4, 2, 2, 2, n_tok // 2), ("y", "xh", "core", "xl", "z")
    )
    return jax.shard_map(
        on_device,
        mesh=fine,
        in_specs=(
            P(None, TOK, None),
            P(None, TOK, FEAT),
            P(None, TOK, None),
            P(None, TOK, None),
            P(None, TOK),
            P(None, None, FEAT),
            P(None, None, FEAT),
            P(TOK, FEAT),
            P(TOK, FEAT),
        ),
        out_specs=(
            P(None, TOK, FEAT),
            P(None, TOK, FEAT),
            P(None, TOK, FEAT),
            P(TOK, FEAT),
            P(TOK, FEAT),
        ),
        check_vma=False,
    )
```

```python
import math

import jax
import jax.numpy as jnp
from jax import lax
from jax.experimental import pallas as pl
from jax.experimental.pallas import tpu as pltpu
from jax.sharding import Mesh, PartitionSpec as P

momentum_decay = 0.9
F32 = jnp.float32
BF16 = jnp.bfloat16

FEAT = ("y", "xh", "core")
TOK = ("xl", "z")
PLANE = FEAT + ("xl",)


def silu_terms(hidden):
    sig = jax.nn.sigmoid(hidden)
    slope = sig * (1.0 + hidden * (1.0 - sig))
    curve = sig * (1.0 - sig) * (2.0 + hidden * (1.0 - 2.0 * sig))
    return (hidden * sig, slope, curve)


def mm(a, b):
    return jnp.dot(a, b, preferred_element_type=F32)


def mm_t(a, b):
    return lax.dot_general(a, b, (((1,), (1,)), ((), ())), preferred_element_type=F32)


def t_mm(a, b):
    return lax.dot_general(a, b, (((0,), (0,)), ((), ())), preferred_element_type=F32)


def swap(x, axis):
    return lax.ppermute(x, axis, [(0, 1), (1, 0)])


def in_order(index, mine, other, axis):
    first = jnp.where(index == 0, mine, other)
    second = jnp.where(index == 0, other, mine)
    return jnp.concatenate([first, second], axis=axis)


def shape(dims, dtype):
    return jax.ShapeDtypeStruct(dims, dtype)


def quarters_of(dims, itemsize):
    part = dims[0] // 4
    if math.prod(dims) * itemsize < 1 << 19 or dims[0] % 4 or (len(dims) == 2 and part % 16):
        return [None]
    return [pl.ds(i * part, part) for i in range(4)]


def call(body, name, flops, out_shapes, operands, scratch=()):
    operands = [x if isinstance(x, tuple) else (x, x.shape, None) for x in operands]
    n, m = len(operands), len(out_shapes)
    total = sum(x.size * x.dtype.itemsize for x in [y[0] for y in operands] + list(out_shapes))

    def kernel(*refs):
        sources, targets = refs[:n], refs[n : n + m]
        held, out = refs[n + m : 2 * n + m], refs[2 * n + m : 2 * n + 2 * m]
        in_sems, out_sems = refs[2 * n + 2 * m : 2 * n + 2 * m + 2]
        rest = refs[2 * n + 2 * m + 2 :]
        copies = []
        count = 0
        for i, (unused, unused_dims, pieces) in enumerate(operands):
            copies.append([])
            if pieces is None:
                whole_of = quarters_of(sources[i].shape, sources[i].dtype.itemsize)
                parts = [(sources[i] if at is None else sources[i].at[at], at) for at in whole_of]
            else:
                parts = pieces(sources[i])
            for source, at in parts:
                target = held[i] if at is None else held[i].at[at]
                copies[i].append(pltpu.make_async_copy(source, target, in_sems.at[count]))
                copies[i][-1].start()
                count += 1
        here = set()
        sent = []

        def take(i, piece=None):
            for p in range(len(copies[i])) if piece is None else [piece]:
                if (i, p) not in here:
                    copies[i][p].wait()
                    here.add((i, p))
            return held[i]

        def give(i, at=None, source_at=None):
            source = out[i] if at is None else out[i].at[at if source_at is None else source_at]
            target = targets[i] if at is None else targets[i].at[at]
            sent.append(pltpu.make_async_copy(source, target, out_sems.at[len(sent)]))
            sent[-1].start()

        body(take, out, give, *rest)
        for i in range(n):
            take(i)
        for copy in sent:
            copy.wait()

    return pl.pallas_call(
        kernel,
        name=name,
        out_shape=list(out_shapes),
        in_specs=[pl.BlockSpec(memory_space=pltpu.HBM)] * n,
        out_specs=[pl.BlockSpec(memory_space=pltpu.HBM)] * m,
        scratch_shapes=[pltpu.VMEM(dims, x.dtype) for x, dims, unused in operands]
        + [pltpu.VMEM(x.shape, x.dtype) for x in out_shapes]
        + [pltpu.SemaphoreType.DMA((64,)), pltpu.SemaphoreType.DMA((64,))]
        + list(scratch),
        compiler_params=pltpu.CompilerParams(vmem_limit_bytes=64 << 20),
        cost_estimate=pl.CostEstimate(flops=flops, bytes_accessed=total, transcendentals=0),
    )(*[x for x, unused, unused_pieces in operands])


def weight(array, u, n_z):
    rows, half = array.shape[3], array.shape[4] // 2

    def pieces(ref):
        cols = pl.ds(pl.multiple_of(lax.axis_index("xl") * half, half), half)
        return [(ref.at[u, x, :, :, cols], (slice(None), x)) for x in range(2)]

    return array, (n_z, 2, rows, half), pieces


def flat(ref):
    n_z, two, rows, half = ref.shape
    return ref[...].reshape(n_z * two * rows, half)


def flat_block(ref, z):
    return ref[z].reshape(-1, ref.shape[3])


def layer(panels, which):
    n_z, both, block = panels.shape
    half = both // 2
    at = pl.ds(which * half, half)
    part = n_z // 2
    return panels, (n_z, half, block), lambda ref: [
        (ref.at[pl.ds(i * part, part), at], pl.ds(i * part, part)) for i in range(2)
    ]


def slot_of(got, slot):
    n, unused, tokens, share = got.shape
    part = n // 4
    return got, (n, tokens, share), lambda ref: [
        (ref.at[pl.ds(i * part, part), slot], pl.ds(i * part, part)) for i in range(4)
    ]


def gathered(got):
    return [slot_of(x, 0) for x in (got if isinstance(got, tuple) else [got])]


def lay_in_all(take, count, rows):
    if count == 1:
        lay_in(take, 0, rows)
        return
    core = lax.axis_index("core")
    lay_in(take, 0, rows, core)
    lay_in(take, 1, rows, 1 - core)


def scaled(rates, u, tokens, share, n_z):
    row = rates[u : u + 1, :] / (2 * tokens * n_z)
    return jnp.broadcast_to(row, (share, tokens)).T


def row_of(array, u):
    dims = array.shape[1:]
    return array, dims, lambda ref: [
        (ref.at[u], None) if at is None else (ref.at[u, at], at)
        for at in quarters_of(dims, array.dtype.itemsize)
    ]


def lay_out(part, chunks, slot, z):
    n_z = chunks.shape[0] // 4
    tokens, share = part.shape[0] // 2, part.shape[1] // 2
    for x in range(2):
        for t in range(2):
            chunks[(x * n_z + z) * 2 + t, slot] = part[
                t * tokens : (t + 1) * tokens, x * share : (x + 1) * share
            ]


def sent_rows(z, n_z):
    return [pl.ds((x * n_z + z - 1) * 2, 4) for x in range(2)] if z % 2 else []


def lay_in(take, i, rows, core=None):
    got = take(i, 0)
    if core is not None:
        n_z = got.shape[0] // 2
        tokens, share = got.shape[1:]
        for chunk in range(got.shape[0]):
            take(i, 4 * chunk // got.shape[0])
            chip, t = chunk // 2, chunk % 2
            z_pair, x = chip % (n_z // 2), chip // (n_z // 2)
            at = pl.multiple_of((4 * z_pair + 2 * core + x) * share, share)
            rows[t * tokens : (t + 1) * tokens, pl.ds(at, share)] = got[chunk]
        return
    n_z = got.shape[0] // 4
    tokens, share = got.shape[1:]
    for x in range(2):
        for z in range(n_z):
            for t in range(2):
                chunk = (x * n_z + z) * 2 + t
                take(i, chunk // n_z)
                at = (2 * z + x) * share
                rows[t * tokens : (t + 1) * tokens, at : at + share] = got[chunk]


def errors(key_rows, w_first, w_second, share):
    updates, tokens, width = key_rows.shape
    full = w_first.shape[2]
    dims = (width // share, updates, tokens, share)
    order = list(reversed(range(updates)))

    def body(take, out, give):
        chunks = out[0]
        for i, u in enumerate(order):
            pre = mm(take(3 * i)[...], take(3 * i + 1)[...])
            act = (pre * jax.nn.sigmoid(pre)).astype(BF16)
            predicted = mm_t(act, take(3 * i + 2)[...]).astype(BF16)
            for f in range(dims[0]):
                chunks[f, u] = predicted[:, f * share : (f + 1) * share]
        for f in range(0, dims[0], 4):
            give(0, pl.ds(f, 4))

    return call(
        body,
        "errors",
        4 * key_rows.size * full,
        [shape(dims, BF16)],
        [row_of(x, u) for u in order for x in (key_rows, w_first, w_second)],
    )[0]


def weigh_out(got, values, rates, chips, n_z):
    n, updates, tokens, share = got.shape

    def body(take, out, give):
        parts, spread_out = out
        terms, value, rate = take(0), take(1), take(2)
        for u in reversed(range(updates)):
            total = terms[0, u].astype(F32)
            for i in range(1, n):
                total += terms[i, u].astype(F32)
            error = total - value[u].astype(F32)
            rounded = (scaled(rate, u, tokens, share, n_z) * error).astype(BF16)
            parts[u] = rounded
            if u == updates - 1:
                for i in range(8):
                    spread_out[i, 0] = rounded
                for i in range(0, chips, 8):
                    give(1, pl.ds(i, 8), pl.ds(0, 8))
        give(0)

    return call(
        body,
        "weigh_out",
        got.size,
        [shape(values.shape, BF16), shape((chips, 1, tokens, share), BF16)],
        [got, values, rates],
    )


def outgoing(arrays, u, finals=()):
    n = len(arrays)
    tokens, width = arrays[0].shape[1:]
    quarter = width // 4

    def quarters(ref):
        core = lax.axis_index("core")
        parts = []
        for side in range(2):
            at = pl.multiple_of(core * (2 * quarter) + side * quarter, quarter)
            parts.append((ref.at[u, :, pl.ds(at, quarter)], side))
        return parts

    def body(take, out, give):
        xl = lax.axis_index("xl")
        for i in range(len(finals)):
            half = finals[i].shape[1] // 2
            both = take(i)[...].astype(F32).T.astype(BF16)
            for which in range(2):
                part = both[which * half : (which + 1) * half]

                @pl.when(xl == which)
                def keep(i=i, half=half, part=part):
                    out[3][i * half : (i + 1) * half, :] = part

                @pl.when(xl != which)
                def send(i=i, half=half, part=part):
                    out[2][i * half : (i + 1) * half, :] = part

        if finals:
            give(2)
            give(3)
        for i in range(n):
            for side in range(2):
                out[side][i] = take(len(finals) + i, side)[side]
        give(0)
        give(1)

    turned = [shape((sum(x.shape[1] // 2 for x in finals), finals[0].shape[0]), BF16)] if finals else []
    return call(
        body,
        "outgoing",
        n * tokens * width,
        [shape((n, tokens, quarter), BF16)] * 2 + turned * 2,
        list(finals) + [(x, (2, tokens, quarter), quarters) for x in arrays],
    )


def incoming(to_right, to_left):
    n = lax.axis_size("xh") * 2
    return (
        lax.ppermute(to_right, ("xh", "xl"), [(i, (i + 1) % n) for i in range(n)]),
        lax.ppermute(to_left, ("xh", "xl"), [(i, (i - 1) % n) for i in range(n)]),
    )


def from_core(pieces):
    return swap(jnp.concatenate(pieces, axis=2), "core")


def whole(arrays, u, pieces, swapped, n_z):
    from_left, from_right = pieces
    n = len(arrays)
    tokens, width = arrays[0].shape[1:]
    share = width // (2 * n_z)
    quarter, half = from_left.shape[2], swapped.shape[2]

    def body(take, out, give):
        full = out[0]
        core = lax.axis_index("core")
        xl = lax.axis_index("xl")
        mine = pl.ds(pl.multiple_of(xl * tokens, tokens), tokens)
        other = pl.ds(pl.multiple_of((1 - xl) * tokens, tokens), tokens)
        for i in range(n):
            for x in range(2):
                for z in range(n_z):
                    at = (2 * z + x) * share
                    block = x * half + z * share
                    full[i, mine, at : at + share] = take(i)[:, block : block + share]
            for z in range(n_z):
                at = z * share
                if at < quarter:
                    piece = take(n)[i, :, at : at + share]
                else:
                    piece = take(n + 1)[i, :, at - quarter : at - quarter + share]
                place = pl.multiple_of((2 * z + core) * share, share)
                full[i, other, pl.ds(place, share)] = piece
                place = pl.multiple_of((2 * z + 1 - core) * share, share)
                full[i, other, pl.ds(place, share)] = take(n + 2)[i, :, at : at + share]
            give(0, i)

    return call(
        body,
        "assemble",
        n * tokens * width,
        [shape((n, 2 * tokens, width), BF16)],
        [row_of(x, u) for x in arrays] + [from_left, from_right, swapped],
    )[0]


def forward(held, inner, u):
    tokens, width = held.shape[1:]
    half = inner.shape[4] // 2
    n_z = inner.shape[2]

    def body(take, out, give):
        act, slope, curve = silu_terms(mm(take(0)[...], flat(take(1))))
        for i, value in enumerate([act.astype(BF16), act.T.astype(BF16), slope, curve]):
            out[i][...] = value
            give(i)

    hidden = (tokens, half)
    return call(
        body,
        "forward",
        2 * tokens * width * half,
        [shape(hidden, BF16), shape((half, tokens), BF16), shape(hidden, F32), shape(hidden, F32)],
        [row_of(held, 0), weight(inner, u, n_z)],
    )


def read_out(held, inner, outer, u):
    tokens, width = held.shape[1:]
    half = inner.shape[4] // 2
    n_z = inner.shape[2]

    def body(take, out, give):
        read, slope, unused = silu_terms(mm(take(0)[...], flat(take(2))))
        back_read = mm(take(1)[...], flat(take(3))) * slope
        values = [read.T.astype(BF16), back_read.astype(BF16), back_read.T.astype(BF16)]
        for i, value in enumerate(values):
            out[i][...] = value
            give(i)

    turned = shape((half, tokens), BF16)
    return call(
        body,
        "read_out",
        4 * tokens * width * half,
        [turned, shape((tokens, half), BF16), turned],
        [row_of(held, 1), row_of(held, 2), weight(inner, u, n_z), weight(outer, u, n_z)],
    )


def weigh_in(got, outer, slope, u):
    n_z = outer.shape[2]
    tokens, half = slope.shape
    width = 2 * n_z * outer.shape[3]
    sources = gathered(got)
    count = len(sources)

    def body(take, out, give):
        rows, gated, delta = out
        lay_in_all(take, count, rows)
        give(0)
        total = mm(rows[...], flat(take(count)))
        gated[...] = total
        give(1)
        delta[...] = (total * take(count + 1)[...]).astype(BF16)
        give(2)

    return call(
        body,
        "weigh_in",
        2 * tokens * width * half,
        [shape((tokens, width), BF16), shape((tokens, half), F32), shape((tokens, half), BF16)],
        sources + [weight(outer, u, n_z), slope],
    )


def back(panels, held, slope, act, outer, chunk_shape, u):
    n_z, both, block = panels.shape
    half = both // 2
    tokens = slope.shape[0]

    def body(take, out, give):
        back_delta, back_gated, chunks = out
        rows = take(0)
        total = jnp.zeros((tokens, half), F32)
        for z in range(n_z):
            total += mm_t(rows[:, z * block : (z + 1) * block], take(1, 2 * z // n_z)[z])
        back_delta[...] = total
        give(0)
        gated_b = (total * take(2)[...]).astype(BF16)
        back_gated[...] = gated_b
        give(1)
        act_in, outer_in = take(3)[...], take(4)
        for z in range(n_z):
            part = mm(act_in, take(5, 2 * z // n_z)[z]) + mm_t(gated_b, flat_block(outer_in, z))
            lay_out(part.astype(BF16), chunks, 0, z)
            for rows_out in sent_rows(z, n_z):
                give(2, rows_out)

    hidden = (tokens, half)
    return call(
        body,
        "back",
        6 * held.shape[2] * tokens * half,
        [shape(hidden, F32), shape(hidden, BF16), shape(chunk_shape, BF16)],
        [row_of(held, 0), layer(panels, 0), slope, act, weight(outer, u, n_z), layer(panels, 1)],
    )


def sum_error(got, rates, u, n_z):
    n, unused, tokens, share = got.shape

    def body(take, out, give):
        part, spread_out = out
        total = jnp.zeros((tokens, share), F32)
        for i in range(n):
            total += take(0, i * 4 // n)[i].astype(F32)
        rounded = (scaled(take(1), u, tokens, share, n_z) * total).astype(BF16)
        part[...] = rounded
        give(0)
        for i in range(8):
            spread_out[i, 0] = rounded
        for i in range(0, n // 2, 8):
            give(1, pl.ds(i, 8), pl.ds(0, 8))

    return call(
        body,
        "error",
        n * tokens * share,
        [shape((tokens, share), BF16), shape((n // 2, 1, tokens, share), BF16)],
        [slot_of(got, 0), rates],
    )


def base_of(
    panels, weighted, slope, curve, back_delta, gated, back_gated, held, read_t, back_read_t
):
    n_z, both, block = panels.shape
    tokens, half = slope.shape

    def body(take, out, give):
        pre, terms = out
        rows = take(0)
        total = jnp.zeros((tokens, half), F32)
        for z in range(n_z):
            total += mm_t(rows[:, z * block : (z + 1) * block], take(1, 2 * z // n_z)[z])
        pre[...] = total * take(2)[...] + take(3)[...] * take(4)[...] * take(5)[...]
        give(0)
        back_gated_t = take(6)[...].astype(F32).T.astype(BF16)
        read_in, back_read_in = take(7)[...], take(8)[...]
        reads, cots = take(9), take(10)
        for z in range(n_z):
            cols = slice(z * block, (z + 1) * block)
            terms[z, :half, :] = mm(back_read_in, reads[:, cols]).astype(BF16)
            second = mm(back_gated_t, rows[:, cols]) + mm(read_in, cots[:, cols])
            terms[z, half:, :] = second.astype(BF16)
            give(1, z)

    return call(
        body,
        "base",
        4 * weighted.size * both,
        [shape(slope.shape, F32), shape(panels.shape, BF16)],
        [weighted, layer(panels, 1), slope, curve, back_delta, gated, back_gated]
        + [read_t, back_read_t, row_of(held, 1), row_of(held, 2)],
    )


def terms_of(got, base_pre, base_terms, slope, outer, held, act_t, u):
    tokens, half = slope.shape
    n_z = outer.shape[2]
    width = held.shape[2]
    block = width // n_z
    sources = gathered(got)
    count = len(sources)

    def body(take_any, out, give, back_out):
        back_pre, terms = out
        lay_in_all(take_any, count, back_out)

        def take(i):
            return take_any(count + i)

        pre = take(2)[...] + mm(back_out[...], flat(take(0))) * take(1)[...]
        back_pre[...] = pre.astype(BF16)
        give(0)
        pre_t = pre.T.astype(BF16)
        act_in, key = take(3)[...], take(4)
        parts = len(quarters_of(base_terms.shape, 2))
        for z in range(n_z):
            cols = slice(z * block, (z + 1) * block)
            base = take_any(count + 5, z * parts // n_z)
            first = mm(pre_t, key[:, cols]) + base[z, :half, :].astype(F32)
            terms[z, :half, :] = first.astype(BF16)
            second = mm(act_in, back_out[:, cols]) + base[z, half:, :].astype(F32)
            terms[z, half:, :] = second.astype(BF16)
            give(1, z)

    return call(
        body,
        "terms",
        6 * tokens * width * half,
        [shape((tokens, half), BF16), shape((n_z, 2 * half, block), BF16)],
        sources
        + [weight(outer, u, n_z), slope, base_pre, act_t, row_of(held, 0), base_terms],
        scratch=[pltpu.VMEM((tokens, width), BF16)],
    )


def spread(parts, n_z, share):
    operands = []
    for part in parts:
        if isinstance(part, list):
            for pair in part:
                operands.extend(pair)
        else:
            operands.append(part)
    tokens = share
    dims = (4 * n_z, len(parts), tokens, share)

    def body(take, out, give):
        chunks = out[0]
        for z in range(n_z):
            at = 0
            for slot, part in enumerate(parts):
                if not isinstance(part, list):
                    for x in range(2):
                        for t in range(2):
                            chunks[(x * n_z + z) * 2 + t, slot] = take(at)[...]
                    at += 1
                    continue
                total = None
                for rows, operand in part:
                    if len(operand[1]) == 3:
                        term = mm(take(at)[...], take(at + 1, 2 * z // n_z)[z])
                    else:
                        term = mm_t(take(at)[...], flat_block(take(at + 1), z))
                    total = term if total is None else total + term
                    at += 2
                lay_out(total.astype(BF16), chunks, slot, z)
            for rows_out in sent_rows(z, n_z):
                give(0, rows_out)

    flops = sum(4 * tokens * math.prod(x[1]) for x in operands if isinstance(x, tuple))
    return call(body, "spread", flops, [shape(dims, BF16)], operands)[0]


def exchange(chunks):
    return lax.all_to_all(chunks, PLANE, 0, 0, tiled=True)


def gather(chunks, beside):
    mine = after(lax.all_to_all(chunks, ("y", "xh", "xl"), 0, 0, tiled=True), beside)
    return mine, swap(mine, "core")


def summed(got, slot):
    return jnp.sum(got[:, slot].astype(F32), axis=0)


def after(value, other):
    return lax.optimization_barrier((value, other))[0]


def on_device(
    key_rows,
    value_rows,
    queries,
    output_cot,
    token_rates,
    w_first,
    w_second,
    final_first,
    final_second,
):
    updates, own_tokens, d_width = key_rows.shape
    share = value_rows.shape[2]
    half = w_first.shape[2] // 2
    n_z = lax.axis_size("z")
    xl = lax.axis_index("xl")
    last = updates - 1
    plane = lax.axis_size(PLANE)

    def part_of(total, which):
        return lax.dynamic_index_in_dim(total.reshape(2 * half, 2, -1), which, 1, keepdims=False)

    inner = w_first.reshape(updates, 2, n_z, -1, 2 * half)
    outer = w_second.reshape(updates, 2, n_z, -1, 2 * half)

    rows = [key_rows, queries, output_cot]

    to_right, to_left, other_final, own_final = outgoing(rows, last, [final_first, final_second])
    pieces = incoming(to_right, to_left)
    other_final = swap(other_final, "xl")
    error_chunks = errors(key_rows, w_first, w_second, share)
    other_final = after(other_final, (error_chunks, pieces))
    start = in_order(xl, own_final, other_final, 1)
    panels = lax.all_gather(-start, "z", axis=0, tiled=False)

    got = lax.all_to_all(after(error_chunks, start), FEAT, 0, 0, tiled=True)
    weighted_part, chunks = weigh_out(got, value_rows, token_rates, plane // 2, n_z)
    held = [None] * updates
    hidden = [None] * updates
    read_list = [None] * updates
    swapped = after(from_core(pieces), weighted_part)
    held[last] = whole(rows, last, pieces, swapped, n_z)
    hidden[last] = forward(held[last], inner, last)
    got = gather(chunks, hidden[last])
    read_list[last] = read_out(after(held[last], panels), inner, outer, last)

    next_in = weigh_in(got, outer, hidden[last][2], last)
    carry = start.astype(F32)
    moment = carry
    totals = []
    parts_sent = []
    key_list = [None] * updates
    value_list = [None] * updates
    query_list = [None] * updates
    for u in reversed(range(updates)):
        act, act_t, slope, curve = hidden[u]
        weighted, gated, delta = next_in
        back_delta, back_gated, chunks = back(
            panels, held[u], slope, act, outer, (plane, 1, own_tokens, share), u
        )
        read_t, back_read, back_read_t = read_list[u]
        base_pre, base_terms = base_of(
            panels,
            weighted,
            slope,
            curve,
            back_delta,
            gated,
            back_gated,
            held[u],
            read_t,
            back_read_t,
        )
        got = after(exchange(after(chunks, got)), (gated, read_list[u]))
        back_part, chunks = sum_error(got, token_rates, u, n_z)
        value_list[u] = -back_part
        beside = [base_pre, base_terms]
        if u > 0:
            chunks_now = spread(
                [
                    (weighted_part, (own_tokens, share), lambda ref: [(ref.at[u - 1], None)]),
                    [(back_read, weight(inner, u, n_z))],
                ],
                n_z,
                share,
            )
            beside.append(chunks_now)
        got = gather(chunks, beside)
        back_pre, terms = terms_of(
            got, base_pre, base_terms, slope, outer, held[u], act_t, u
        )
        key_parts = [(delta, layer(panels, 0)), (back_pre, weight(inner, u, n_z))]
        total = lax.psum_scatter(terms, "z", scatter_dimension=0, tiled=True)[0]
        if u > 0:
            got = exchange(after(chunks_now, terms))
            chunks = spread([key_parts], n_z, share)
            sent = outgoing([after(x, terms) for x in rows], u - 1)
            total, got, chunks, sent = lax.optimization_barrier((total, got, chunks, sent))
            totals.append(total)
            carry = carry + total.astype(F32)
            moment = carry + momentum_decay * moment
            panel = (-moment).astype(BF16)
            panels = lax.all_gather(panel, "z", axis=0, tiled=False)
            pieces = incoming(*[after(x, panel) for x in sent])
            swapped = from_core(pieces)
            sums = exchange(after(chunks, swapped))
            held[u - 1] = whole(rows, u - 1, pieces, swapped, n_z)
            query_list[u] = summed(after(got, panel), 1).astype(BF16)
            hidden[u - 1] = forward(held[u - 1], inner, u - 1)
            read_list[u - 1] = read_out(held[u - 1], inner, outer, u - 1)
            next_in = weigh_in(after(got, panel), outer, hidden[u - 1][2], u - 1)
            leaving = part_of(total, 1 - xl)
            panels, sums, next_in, leaving = lax.optimization_barrier(
                (panels, sums, next_in, leaving)
            )
            parts_sent.append(leaving)
            key_list[u] = summed(sums, 0).astype(BF16)
        else:
            parts = [key_parts, [(back_read, weight(inner, u, n_z))]]
            chunks = spread(parts, n_z, share)
            sent = [swap(after(x, terms), "xl") for x in parts_sent]
            sums = exchange(after(chunks, sent))
            totals.append(total)
            sent.append(swap(part_of(total, 1 - xl), "xl"))
            key_list[u] = summed(sums, 0).astype(BF16)
            query_list[u] = summed(sums, 1).astype(BF16)

    grad_first = final_first.astype(F32)
    grad_second = final_second.astype(F32)
    for total, other in zip(totals, sent):
        kept, other = part_of(total, xl).T, other.T
        grad_first = grad_first + in_order(xl, kept[:, :half], other[:, :half], 1)
        grad_second = grad_second + in_order(xl, kept[:, half:], other[:, half:], 1)
    return (
        jnp.stack(key_list),
        jnp.stack(value_list),
        jnp.stack(query_list),
        grad_first,
        grad_second,
    )


def solution(mesh):
    n_feat, n_tok = mesh.devices.shape
    fine = Mesh(
        mesh.devices.reshape(n_feat // 4, 2, 2, 2, n_tok // 2), ("y", "xh", "core", "xl", "z")
    )
    return jax.shard_map(
        on_device,
        mesh=fine,
        in_specs=(
            P(None, TOK, None),
            P(None, TOK, FEAT),
            P(None, TOK, None),
            P(None, TOK, None),
            P(None, TOK),
            P(None, None, FEAT),
            P(None, None, FEAT),
            P(TOK, FEAT),
            P(TOK, FEAT),
        ),
        out_specs=(
            P(None, TOK, FEAT),
            P(None, TOK, FEAT),
            P(None, TOK, FEAT),
            P(TOK, FEAT),
            P(TOK, FEAT),
        ),
        check_vma=False,
    )
```
